32 devices in a mesh: replica: 4 (over x, core), inner: 8 (over z, y).
Axes of the slice: x: 2, y: 2, z: 4, core: 2. Of those that a mesh axis runs over, the one named last changes fastest.
Arguments:
- square_weights: float32 [2, 1024, 1024], P(None, 'inner'), may hold values from -6 to 6
- square_copies: float32 [4, 2, 1024, 1024], P('replica', None, 'inner'), may hold values from -6 to 6
- square_moment: float32 [2, 1024, 1024], P(None, 'inner'), may hold values from -6 to 6
- broad_weights: float32 [2, 1024, 2048], P(None, 'inner'), may hold values from -6 to 6
- broad_copies: float32 [4, 2, 1024, 2048], P('replica', None, 'inner'), may hold values from -6 to 6
- broad_moment: float32 [2, 1024, 2048], P(None, 'inner'), may hold values from -6 to 6
- embed_weights: float32 [16384, 1024], P('inner'), may hold values from -6 to 6
- embed_copies: float32 [4, 16384, 1024], P('replica', 'inner'), may hold values from -90 to 90, as said below
- embed_moment: float32 [16384, 1024], P('inner'), may hold values from -6 to 6
- embed_error: float32 [4, 16384, 1024], P('replica', 'inner'), may hold values from -3 to 3
- warm_start: float32 [64, 1024], replicated, may hold values from -6 to 6
Outputs:
- square_updated: float32 [2, 1024, 1024], P(None, 'inner')
- square_velocity: float32 [2, 1024, 1024], P(None, 'inner')
- broad_updated: float32 [2, 1024, 2048], P(None, 'inner')
- broad_velocity: float32 [2, 1024, 2048], P(None, 'inner')
- embed_updated: float32 [16384, 1024], P('inner')
- embed_velocity: float32 [16384, 1024], P('inner')
- embed_carried: float32 [4, 16384, 1024], P('replica', 'inner')
The draws below stay inside these ranges and needn't reach their ends.
Inputs may be any that keep to these rules, and one draw needn't show every extreme that they name: `embed_copies`: each replica's embedding after its inner steps.
All inputs are finite; a program needn't handle non-finite values.
Results may differ from the reference program's by a relative error of at most 0.0001.
Values sent between devices are 32-bit elements; how exact they have to be, the bound alone decides.
No kernel may reach another device: no remote copies, remote signals or barrier semaphores. Data moves between devices by JAX's collectives and lax.ppermute only.
A program may use at most 128 MiB of HBM per device.

```python
import math
import jax
import jax.numpy as jnp
from jax import lax

D = 1024
VDIM = 2048
VOCAB = 16384
RANK = 64
REPLICAS = 4


def embed_parts(key):
    base = jax.random.truncated_normal(jax.random.fold_in(key, 101), -6.0, 6.0, (VOCAB, D), jnp.float32)
    noise = jax.random.truncated_normal(jax.random.fold_in(key, 103), -6.0, 6.0, (REPLICAS, VOCAB, D), jnp.float32)
    rough = jax.random.uniform(jax.random.fold_in(key, 102), (VOCAB, 1), jnp.float32, 0.5, 1.0)
    ramp = jnp.arange(VOCAB, dtype=jnp.float32) / max(VOCAB - 1, 1)
    row_scale = 0.3 * jnp.exp(ramp * math.log(10.0))[:, None] * rough
    delta = row_scale * noise
    return (base, base[None] - delta)


def draw_embed_weights(key, part):
    return embed_parts(key)[0]


def draw_embed_copies(key, part):
    return embed_parts(key)[1]


def draw_warm_start(key, part):
    values = jax.random.truncated_normal(jax.random.fold_in(key, 201), -6.0, 6.0, (RANK, D), jnp.float32)
    spread = math.log(10.0)
    scales = jnp.exp(jax.random.uniform(jax.random.fold_in(key, 202), (RANK, 1), jnp.float32, 0.0, spread))
    return values * scales / 32.0


def block_scale(own_key, dims, split, smallest, top_value):
    def one(axis_at, parts):
        steps = jax.random.uniform(jax.random.fold_in(jax.random.fold_in(own_key, 6), axis_at), (parts,), jnp.float32, smallest / len(split), top_value / len(split))
        return jnp.repeat(jnp.exp(steps), dims[axis_at] // parts).reshape((-1,) + (1,) * (len(dims) - axis_at - 1))

    factor_of = one(*split[0])
    for cut in split[1:]:
        factor_of = factor_of * one(*cut)
    return factor_of


def centred(stream_key, shape, width, limit, pieces=(), held_as=jnp.bfloat16):
    entries = width * jax.random.normal(stream_key, shape, jnp.float32)
    if pieces:
        entries = entries * block_scale(stream_key, shape, pieces, -0.22, 0.18)
    return jnp.clip(entries, -limit, limit).astype(held_as)


def setup_inputs(seed: int = 0) -> dict:
    splits = jax.random.split(jax.random.key(seed), 12)
    square_weights = centred(splits[0], (2, D, D), 1.0, 6.0, ((1, 8),), jnp.float32)
    square_copies = centred(splits[1], (REPLICAS, 2, D, D), 1.0, 6.0, ((0, 4), (2, 8)), jnp.float32)
    square_moment = centred(splits[2], (2, D, D), 1.0, 6.0, ((1, 8),), jnp.float32)
    broad_weights = centred(splits[3], (2, D, VDIM), 1.0, 6.0, ((1, 8),), jnp.float32)
    broad_copies = centred(splits[4], (REPLICAS, 2, D, VDIM), 1.0, 6.0, ((0, 4), (2, 8)), jnp.float32)
    broad_moment = centred(splits[5], (2, D, VDIM), 1.0, 6.0, ((1, 8),), jnp.float32)
    embed_weights = draw_embed_weights(jax.random.fold_in(splits[11], 71), 0)
    embed_copies = draw_embed_copies(jax.random.fold_in(splits[11], 71), 0)
    embed_moment = centred(splits[8], (VOCAB, D), 1.0, 6.0, ((0, 8),), jnp.float32)
    embed_error = centred(splits[9], (REPLICAS, VOCAB, D), 0.5, 3.0, ((0, 4), (1, 8)), jnp.float32)
    warm_start = draw_warm_start(jax.random.fold_in(splits[11], 71), 0)
    return dict(square_weights=square_weights, square_copies=square_copies, square_moment=square_moment, broad_weights=broad_weights, broad_copies=broad_copies, broad_moment=broad_moment, embed_weights=embed_weights, embed_copies=embed_copies, embed_moment=embed_moment, embed_error=embed_error, warm_start=warm_start)


outer_rate = 0.7
momentum_decay = 0.9

def nesterov(weights, gradient, moment):
    velocity = momentum_decay * moment + gradient
    return (weights - outer_rate * (gradient + momentum_decay * velocity), velocity)

def reference(square_weights, square_copies, square_moment, broad_weights, broad_copies, broad_moment, embed_weights, embed_copies, embed_moment, embed_error, warm_start):
    highest = lax.Precision.HIGHEST
    contract_last = (((1,), (1,)), ((), ()))
    square_mean = jnp.sum(square_weights[None] - square_copies, axis=0) / REPLICAS
    broad_mean = jnp.sum(broad_weights[None] - broad_copies, axis=0) / REPLICAS
    square_updated, square_velocity = nesterov(square_weights, square_mean, square_moment)
    broad_updated, broad_velocity = nesterov(broad_weights, broad_mean, broad_moment)
    corrected = embed_weights[None] - embed_copies + embed_error
    left_factor = jnp.zeros((RANK, VOCAB), jnp.float32)
    for replica in range(REPLICAS):
        left_factor = left_factor + lax.dot_general(warm_start, corrected[replica], contract_last, precision=highest)
    left_factor = left_factor / REPLICAS
    gram_matrix = lax.dot_general(left_factor, left_factor, contract_last, precision=highest)
    lower_factor = jnp.linalg.cholesky(gram_matrix)
    basis_rows = lax.linalg.triangular_solve(lower_factor, left_factor, left_side=True, lower=True)
    right_factor = jnp.zeros((RANK, D), jnp.float32)
    for replica in range(REPLICAS):
        right_factor = right_factor + jnp.dot(basis_rows, corrected[replica], precision=highest)
    right_factor = right_factor / REPLICAS
    embed_step = lax.dot_general(basis_rows, right_factor, (((0,), (0,)), ((), ())), precision=highest)
    embed_carried = corrected - embed_step[None]
    embed_updated, embed_velocity = nesterov(embed_weights, embed_step, embed_moment)
    return (square_updated, square_velocity, broad_updated, broad_velocity, embed_updated, embed_velocity, embed_carried)
```

```python
import jax
import jax.numpy as jnp
from jax import lax
from jax.sharding import PartitionSpec as P

outer_rate = 0.7
momentum_decay = 0.9


def nesterov(weights, gradient, moment):
    velocity = momentum_decay * moment + gradient
    return (weights - outer_rate * (gradient + momentum_decay * velocity), velocity)


def swap(value, axis, bit):
    return lax.ppermute(value, axis, [(i, i ^ bit) for i in range(lax.axis_size(axis))])


def doubled(value, axis, first=1):
    bit = first
    while bit < lax.axis_size(axis):
        value = value + swap(value, axis, bit)
        bit *= 2
    return value


def halved(value):
    core = lax.axis_index("replica") % 2
    away = lax.dynamic_index_in_dim(value, 1 - core, 0, keepdims=True)
    kept = lax.dynamic_index_in_dim(value, core, 0, keepdims=True)
    return kept + swap(away, "replica", 1)


def rejoined(half):
    other = swap(half, "replica", 1)
    first = lax.axis_index("replica") % 2 == 0
    return jnp.concatenate([jnp.where(first, half, other), jnp.where(first, other, half)], axis=0)


def local(
    square_weights,
    square_copies,
    square_moment,
    broad_weights,
    broad_copies,
    broad_moment,
    embed_weights,
    embed_copies,
    embed_moment,
    embed_error,
    warm_start,
):
    replicas = lax.axis_size("replica")
    highest = lax.Precision.HIGHEST
    contract_last = (((1,), (1,)), ((), ()))
    rank, width = warm_start.shape
    corrected = embed_weights - embed_copies[0] + embed_error[0]
    left_local = lax.dot_general(warm_start, corrected, contract_last, precision=highest)
    left_half = doubled(halved(left_local.reshape(2, rank // 2, -1)), "replica", 2)
    left_factor = rejoined(left_half).reshape(rank, -1) / replicas

    square_sum = rejoined(doubled(halved(square_weights - square_copies[0]), "replica", 2))
    broad_sum = rejoined(doubled(halved(broad_weights - broad_copies[0]), "replica", 2))

    gram_local = lax.dot_general(left_factor, left_factor, contract_last, precision=highest)
    right_local = jnp.dot(left_factor, corrected, precision=highest)
    gram_matrix = doubled(gram_local, "inner")
    right_half = halved(right_local.reshape(2, rank // 2, width))
    right_half = doubled(doubled(right_half, "inner"), "replica", 2)
    lower_factor = jnp.linalg.cholesky(gram_matrix)
    basis_rows = lax.linalg.triangular_solve(lower_factor, left_factor, left_side=True, lower=True)
    right_total = rejoined(right_half).reshape(rank, width) / replicas
    right_factor = lax.linalg.triangular_solve(lower_factor, right_total, left_side=True, lower=True)
    embed_step = lax.dot_general(
        basis_rows, right_factor, (((0,), (0,)), ((), ())), precision=highest
    )
    embed_updated, embed_velocity = nesterov(embed_weights, embed_step, embed_moment)
    square_updated, square_velocity = nesterov(square_weights, square_sum / replicas, square_moment)
    broad_updated, broad_velocity = nesterov(broad_weights, broad_sum / replicas, broad_moment)
    embed_carried = (corrected - embed_step)[None]
    return (
        square_updated,
        square_velocity,
        broad_updated,
        broad_velocity,
        embed_updated,
        embed_velocity,
        embed_carried,
    )


def solution(mesh):
    in_specs = (
        P(None, "inner", None),
        P("replica", None, "inner", None),
        P(None, "inner", None),
        P(None, "inner", None),
        P("replica", None, "inner", None),
        P(None, "inner", None),
        P("inner", None),
        P("replica", "inner", None),
        P("inner", None),
        P("replica", "inner", None),
        P(),
    )
    out_specs = (
        P(None, "inner", None),
        P(None, "inner", None),
        P(None, "inner", None),
        P(None, "inner", None),
        P("inner", None),
        P("inner", None),
        P("replica", "inner", None),
    )
    return jax.shard_map(local, mesh=mesh, in_specs=in_specs, out_specs=out_specs, check_vma=False)
```

```python
import functools
import math

import jax
import jax.numpy as jnp
from jax import lax
from jax.experimental import pallas as pl
from jax.experimental.pallas import tpu as pltpu
from jax.sharding import PartitionSpec as P

outer_rate = 0.7
momentum_decay = 0.9
MIB = 1 << 20


def nesterov(weights, gradient, moment):
    velocity = momentum_decay * moment + gradient
    return (weights - outer_rate * (gradient + momentum_decay * velocity), velocity)


def split3(value):
    high = value.astype(jnp.bfloat16)
    rest = value - high.astype(jnp.float32)
    middle = rest.astype(jnp.bfloat16)
    low = (rest - middle.astype(jnp.float32)).astype(jnp.bfloat16)
    return high, middle, low


def stacked_product(parts, right, dims):
    rows = parts.shape[0] // 3
    high, middle, low = split3(right)
    dot = functools.partial(lax.dot_general, dimension_numbers=(dims, ((), ())), preferred_element_type=jnp.float32)
    one = dot(parts, high)
    two = dot(parts[: 2 * rows], middle)
    three = dot(parts[:rows], low)
    small = one[2 * rows :] + two[rows:] + three
    return one[:rows] + (one[rows : 2 * rows] + two[:rows] + small)


def swap(value, axis, bit):
    return lax.ppermute(value, axis, [(i, i ^ bit) for i in range(lax.axis_size(axis))])


def doubled(value, axis, first=1):
    bit = first
    while bit < lax.axis_size(axis):
        value = value + swap(value, axis, bit)
        bit *= 2
    return value


def sum_over_chips(value, after):
    bit = 2
    while bit < lax.axis_size("replica"):
        value = sum_call(value, swap(value, "replica", bit), after)
        bit *= 2
    return value


def in_hbm(value):
    return pltpu.with_memory_space_constraint(value, pltpu.HBM)


def in_vmem(value):
    return pltpu.with_memory_space_constraint(value, pltpu.VMEM)


VMEM = pl.BlockSpec(memory_space=pltpu.VMEM)
SMEM = pl.BlockSpec(memory_space=pltpu.SMEM)
ANY = pl.BlockSpec(memory_space=pl.ANY)


def ordered(first, mine, other):
    return jnp.concatenate([jnp.where(first, mine, other), jnp.where(first, other, mine)], axis=0)


def left_kernel(chunk_after, core, weights, copies, error, warm, *refs):
    corrected, held, away, kept, parts = refs[chunk_after:]
    step = pl.program_id(0)
    rows = weights.shape[0]
    half = away.shape[0]

    @pl.when(step == 0)
    def _():
        first = core[0] == 0
        top, bottom = warm[:half], warm[half:]
        both = jnp.concatenate([jnp.where(first, bottom, top), jnp.where(first, top, bottom)], axis=0)
        parts[...] = jnp.concatenate(split3(both), axis=0)

    value = weights[...] - copies[0] + error[0]
    here = pl.ds(pl.multiple_of(step * rows, rows), rows)
    corrected[here, :] = value
    held[here, :] = weights[...]
    left = stacked_product(parts[...], value, ((1,), (1,)))
    away[...] = left[:half]
    kept[...] = left[half:]


def left_call(core, weights, copies, error, warm, after, start, rows, block):
    rank, width = warm.shape
    first = start // block
    row = lambda i: (first + i, 0)
    lead = lambda i: (0, first + i, 0)
    return pl.pallas_call(
        functools.partial(left_kernel, len(after)),
        grid=(rows // block,),
        in_specs=[
            SMEM,
            pl.BlockSpec((block, width), row),
            pl.BlockSpec((1, block, width), lead),
            pl.BlockSpec((1, block, width), lead),
            VMEM,
        ]
        + [ANY] * len(after),
        out_specs=[
            VMEM,
            VMEM,
            pl.BlockSpec((rank // 2, block), lambda i: (0, i)),
            pl.BlockSpec((rank // 2, block), lambda i: (0, i)),
        ],
        out_shape=[
            pltpu.VMEM((rows, width), jnp.float32),
            pltpu.VMEM((rows, width), jnp.float32),
            jax.ShapeDtypeStruct((rank // 2, rows), jnp.float32),
            jax.ShapeDtypeStruct((rank // 2, rows), jnp.float32),
        ],
        scratch_shapes=[pltpu.VMEM((3 * rank, width), jnp.bfloat16)],
        compiler_params=pltpu.CompilerParams(vmem_limit_bytes=26 * MIB),
        name="left",
    )(core, in_hbm(weights), in_hbm(copies), in_hbm(error), warm, *after)


def right_kernel(scale, block, core, mine, other, corrected, *refs):
    away, kept, left = refs[-3:]
    half, rows = mine.shape
    width = corrected.shape[1]
    first = core[0] == 0
    whole = ordered(first, mine[...] * scale, other[...] * scale)
    left[...] = whole
    parts = jnp.concatenate(split3(whole), axis=0)
    total = None
    for i in range(rows // block):
        cut = slice(i * block, (i + 1) * block)
        term = stacked_product(parts[:, cut], corrected[cut, :], ((1,), (0,)))
        total = term if total is None else total + term
    square = stacked_product(parts, whole, ((1,), (1,)))
    top, bottom = total[:half], total[half:]
    away_value, kept_value = jnp.where(first, bottom, top), jnp.where(first, top, bottom)
    gram = jnp.concatenate([square[:half], square[half:]], axis=1)
    if len(refs) > 3:
        away_before, kept_before = refs[:2]
        away_value = away_value + away_before[:, :width]
        kept_value = kept_value + kept_before[:, :width]
        gram = gram + kept_before[:, width:]
    away[:, :width] = away_value
    away[:, width:] = jnp.zeros_like(gram)
    kept[:, :width] = kept_value
    kept[:, width:] = gram


def right_call(core, mine, other, corrected, before, scale, block):
    half, rows = mine.shape
    width = corrected.shape[1]
    message = jax.ShapeDtypeStruct((half, width + 4 * half), jnp.float32)
    return pl.pallas_call(
        functools.partial(right_kernel, scale, block),
        in_specs=[SMEM] + [VMEM] * (3 + len(before)),
        out_specs=[VMEM] * 3,
        out_shape=[message, message, jax.ShapeDtypeStruct((2 * half, rows), jnp.float32)],
        compiler_params=pltpu.CompilerParams(vmem_limit_bytes=12 * MIB),
        name="right",
    )(core, mine, other, in_vmem(corrected), *before)


def factor_kernel(width, message, *refs):
    chunks = (len(refs) - 1) // 2
    left, inverse, basis = refs[:chunks], refs[chunks], refs[chunks + 1 :]
    half = message.shape[0]
    rank = 2 * half
    pair = message[:, width:]
    gram = jnp.concatenate([pair[:, :rank], pair[:, rank:]], axis=0)
    eye = jnp.where(
        lax.broadcasted_iota(jnp.int32, (rank, rank), 0) == lax.broadcasted_iota(jnp.int32, (rank, rank), 1), 1.0, 0.0
    )
    both = jnp.concatenate([gram, eye], axis=1)
    bands = [both[i : i + 8, :] for i in range(0, rank, 8)]
    for j in range(rank):
        band, line = divmod(j, 8)
        row = bands[band][line : line + 1, :]
        root = lax.rsqrt(row[:, j : j + 1])
        row = row * root
        inverse[j : j + 1, :] = row[:, rank:]
        for i in range(band, rank // 8):
            bands[i] = bands[i] - (bands[i][:, j : j + 1] * root) * row
    for chunk in range(chunks):
        rows = lax.dot_general(
            inverse[...],
            left[chunk][...],
            (((1,), (0,)), ((), ())),
            precision=lax.Precision.HIGHEST,
            preferred_element_type=jnp.float32,
        )
        high, middle, low = split3(rows.T)
        basis[chunk][...] = jnp.concatenate([high, high, middle, high, low, middle], axis=1)


def factor_call(message, left, width):
    half = message.shape[0]
    rank = 2 * half
    return pl.pallas_call(
        functools.partial(factor_kernel, width),
        in_specs=[VMEM] * (1 + len(left)),
        out_specs=[VMEM] * (1 + len(left)),
        out_shape=[jax.ShapeDtypeStruct((rank, rank), jnp.float32)]
        + [jax.ShapeDtypeStruct((piece.shape[1], 6 * rank), jnp.bfloat16) for piece in left],
        compiler_params=pltpu.CompilerParams(vmem_limit_bytes=12 * MIB),
        name="factor",
    )(message, *left)


def final_kernel(scale, chunks, core, mine, other, inverse, moment, *refs):
    weights, corrected, basis = refs[:chunks], refs[chunks : 2 * chunks], refs[2 * chunks : 3 * chunks]
    updated, velocity, carried, parts = refs[3 * chunks :]
    step = pl.program_id(0)
    rows, width = updated.shape
    here = pl.ds(pl.multiple_of(step * rows, rows), rows)

    @pl.when(step == 0)
    def _():
        whole = ordered(core[0] == 0, mine[:, :width] * scale, other[:, :width] * scale)
        right = lax.dot_general(
            inverse[...], whole, (((1,), (0,)), ((), ())), precision=lax.Precision.HIGHEST, preferred_element_type=jnp.float32
        )
        high, middle, low = split3(right)
        parts[...] = jnp.concatenate([high, middle, high, low, high, middle], axis=0)

    def work(chunk, at):
        there = pl.ds(pl.multiple_of(at, rows), rows)
        change = jnp.dot(basis[chunk][there, :], parts[...], preferred_element_type=jnp.float32)
        carried[0] = corrected[chunk][there, :] - change
        new, speed = nesterov(weights[chunk][there, :], change, moment[here, :])
        updated[...] = new
        velocity[...] = speed

    per = corrected[0].shape[0] // rows
    for chunk in range(chunks):
        pl.when(step // per == chunk)(functools.partial(work, chunk, (step - chunk * per) * rows))


def final_call(core, mine, other, inverse, moment, weights, corrected, basis, scale, block):
    rows, width = moment.shape
    rank = inverse.shape[0]
    chunks = len(corrected)
    out = pl.BlockSpec((block, width), lambda i: (i, 0))
    large = [in_vmem(value) for value in (moment, *weights, *corrected, *basis)]
    return pl.pallas_call(
        functools.partial(final_kernel, scale, chunks),
        grid=(rows // block,),
        in_specs=[SMEM] + [VMEM] * (3 + len(large)),
        out_specs=[out, out, pl.BlockSpec((1, block, width), lambda i: (0, i, 0))],
        out_shape=[
            jax.ShapeDtypeStruct((rows, width), jnp.float32),
            jax.ShapeDtypeStruct((rows, width), jnp.float32),
            jax.ShapeDtypeStruct((1, rows, width), jnp.float32),
        ],
        scratch_shapes=[pltpu.VMEM((6 * rank, width), jnp.bfloat16)],
        compiler_params=pltpu.CompilerParams(vmem_limit_bytes=16 * MIB),
        name="final",
    )(core, mine, other, inverse, *large)


def sum_kernel(one, two, *refs):
    refs[-1][...] = one[...] + two[...]


def sum_call(one, two, after):
    return pl.pallas_call(
        sum_kernel,
        in_specs=[VMEM] * 2 + [ANY] * len(after),
        out_specs=VMEM,
        out_shape=jax.ShapeDtypeStruct(one.shape, one.dtype),
        compiler_params=pltpu.CompilerParams(vmem_limit_bytes=8 * MIB),
        name="sum",
    )(one, two, *after)


def term_kernel(core, weights, copies, received, *refs):
    at = core[0]
    refs[-1][0] = (weights[at] - copies[0, at]) + (weights[at] - received[0, at])


def term_call(core, weights, copies, received, after):
    return pl.pallas_call(
        term_kernel,
        in_specs=[SMEM] + [VMEM] * 3 + [ANY] * len(after),
        out_specs=VMEM,
        out_shape=jax.ShapeDtypeStruct((1, *weights.shape[1:]), jnp.float32),
        compiler_params=pltpu.CompilerParams(vmem_limit_bytes=12 * MIB),
        name="term",
    )(core, weights, copies, received, *after)


def layer_kernel(scale, core, mine, other, weights, moment, *refs):
    updated, velocity = refs[-2:]
    for value, at in ((mine, core[0]), (other, 1 - core[0])):
        updated[at], velocity[at] = nesterov(weights[at], value[0] * scale, moment[at])


def layer_call(core, mine, other, weights, moment, after, scale):
    return pl.pallas_call(
        functools.partial(layer_kernel, scale),
        in_specs=[SMEM] + [VMEM] * 4 + [ANY] * len(after),
        out_specs=[VMEM] * 2,
        out_shape=[jax.ShapeDtypeStruct(weights.shape, jnp.float32)] * 2,
        compiler_params=pltpu.CompilerParams(vmem_limit_bytes=16 * MIB),
        name="layer",
    )(core, mine, other, weights, moment, *after)


def local(
    square_weights,
    square_copies,
    square_moment,
    broad_weights,
    broad_copies,
    broad_moment,
    embed_weights,
    embed_copies,
    embed_moment,
    embed_error,
    warm_start,
):
    replicas = lax.axis_size("replica")
    scale = 1 / replicas
    rank, width = warm_start.shape
    rows = embed_weights.shape[0]
    chunks = 2 if rows % 512 == 0 else 1
    size = rows // chunks
    block = math.gcd(size, 256)
    wide = math.gcd(size, 512)
    core = jnp.reshape(lax.axis_index("replica") % 2, (1,)).astype(jnp.int32)

    square_received = swap(square_copies, "replica", 1)
    broad_received = swap(broad_copies, "replica", 1)
    corrected, held, halves, after = [], [], [], ()
    for chunk in range(chunks):
        value, weights, away, kept = left_call(
            core, embed_weights, embed_copies, embed_error, warm_start, after, chunk * size, size, wide
        )
        corrected.append(value)
        held.append(weights)
        halves.append(sum_call(kept, swap(away, "replica", 1), ()))
        if chunk == 0:
            square_half = term_call(core, square_weights, square_copies, square_received, (away,))
            after = (square_half, halves[0])
    left, before = [], ()
    for chunk in range(chunks):
        half = doubled(halves[chunk], "replica", 2)
        other = swap(half, "replica", 1)
        *before, piece = right_call(core, half, other, corrected[chunk], before, scale, block)
        left.append(piece)
    away, kept = before
    broad_half = term_call(core, broad_weights, broad_copies, broad_received, (half,))

    message = sum_call(kept, swap(away, "replica", 1), ())
    inner = lax.axis_size("inner")
    bit = 1
    while bit < inner:
        received = swap(message, "inner", bit)
        after = ()
        if 2 * bit >= inner:
            square_half = sum_over_chips(square_half, (message,))
            square_other = swap(square_half, "replica", 1)
            square_updated, square_velocity = layer_call(
                core, square_half, square_other, square_weights, square_moment, (), scale
            )
            after = (square_velocity,)
        message = sum_call(message, received, after)
        bit *= 2
    inverse, *basis = factor_call(message, left, width)
    right_half = sum_over_chips(message, (inverse,))
    broad_half = sum_over_chips(broad_half, (inverse,))
    broad_other = swap(broad_half, "replica", 1)
    broad_updated, broad_velocity = layer_call(
        core, broad_half, broad_other, broad_weights, broad_moment, (right_half,), scale
    )
    right_other = swap(right_half, "replica", 1)
    embed_updated, embed_velocity, embed_carried = final_call(
        core, right_half, right_other, inverse, embed_moment, held, corrected, basis, scale, block
    )
    return (
        square_updated,
        square_velocity,
        broad_updated,
        broad_velocity,
        embed_updated,
        embed_velocity,
        embed_carried,
    )


def solution(mesh):
    in_specs = (
        P(None, "inner", None),
        P("replica", None, "inner", None),
        P(None, "inner", None),
        P(None, "inner", None),
        P("replica", None, "inner", None),
        P(None, "inner", None),
        P("inner", None),
        P("replica", "inner", None),
        P("inner", None),
        P("replica", "inner", None),
        P(),
    )
    out_specs = (
        P(None, "inner", None),
        P(None, "inner", None),
        P(None, "inner", None),
        P(None, "inner", None),
        P("inner", None),
        P("inner", None),
        P("replica", "inner", None),
    )
    return jax.shard_map(local, mesh=mesh, in_specs=in_specs, out_specs=out_specs, check_vma=False)
```

```python
import functools
import math

import jax
import jax.numpy as jnp
from jax import lax
from jax.experimental import pallas as pl
from jax.experimental.pallas import tpu as pltpu
from jax.sharding import PartitionSpec as P

outer_rate = 0.7
momentum_decay = 0.9
MIB = 1 << 20


def nesterov(weights, gradient, moment):
    velocity = momentum_decay * moment + gradient
    return (weights - outer_rate * (gradient + momentum_decay * velocity), velocity)


def split3(value):
    high = value.astype(jnp.bfloat16)
    rest = value - high.astype(jnp.float32)
    middle = rest.astype(jnp.bfloat16)
    low = (rest - middle.astype(jnp.float32)).astype(jnp.bfloat16)
    return high, middle, low


def stacked_product(parts, right, dims):
    rows = parts.shape[0] // 3
    high, middle, low = split3(right)
    dot = functools.partial(lax.dot_general, dimension_numbers=(dims, ((), ())), preferred_element_type=jnp.float32)
    one = dot(parts, high)
    two = dot(parts[: 2 * rows], middle)
    three = dot(parts[:rows], low)
    small = one[2 * rows :] + two[rows:] + three
    return one[:rows] + (one[rows : 2 * rows] + two[:rows] + small)


def swap(value, axis, bit):
    return lax.ppermute(value, axis, [(i, i ^ bit) for i in range(lax.axis_size(axis))])


def doubled(value, axis, first=1):
    bit = first
    while bit < lax.axis_size(axis):
        value = value + swap(value, axis, bit)
        bit *= 2
    return value


def sum_over_chips(value, after):
    bit = 2
    while bit < lax.axis_size("replica"):
        value = sum_call(value, swap(value, "replica", bit), after)
        bit *= 2
    return value


def in_hbm(value):
    return pltpu.with_memory_space_constraint(value, pltpu.HBM)


def in_vmem(value):
    return pltpu.with_memory_space_constraint(value, pltpu.VMEM)


VMEM = pl.BlockSpec(memory_space=pltpu.VMEM)
SMEM = pl.BlockSpec(memory_space=pltpu.SMEM)
ANY = pl.BlockSpec(memory_space=pl.ANY)


def ordered(first, mine, other):
    return jnp.concatenate([jnp.where(first, mine, other), jnp.where(first, other, mine)], axis=0)


def left_kernel(chunk_after, core, weights, copies, error, warm, *refs):
    corrected, held, away, kept, parts = refs[chunk_after:]
    step = pl.program_id(0)
    rows = weights.shape[0]
    half = away.shape[0]

    @pl.when(step == 0)
    def _():
        first = core[0] == 0
        top, bottom = warm[:half], warm[half:]
        both = jnp.concatenate([jnp.where(first, bottom, top), jnp.where(first, top, bottom)], axis=0)
        parts[...] = jnp.concatenate(split3(both), axis=0)

    value = weights[...] - copies[0] + error[0]
    here = pl.ds(pl.multiple_of(step * rows, rows), rows)
    corrected[here, :] = value
    held[here, :] = weights[...]
    left = stacked_product(parts[...], value, ((1,), (1,)))
    away[...] = left[:half]
    kept[...] = left[half:]


def left_call(core, weights, copies, error, warm, after, start, rows, block):
    rank, width = warm.shape
    first = start // block
    row = lambda i: (first + i, 0)
    lead = lambda i: (0, first + i, 0)
    return pl.pallas_call(
        functools.partial(left_kernel, len(after)),
        grid=(rows // block,),
        in_specs=[
            SMEM,
            pl.BlockSpec((block, width), row),
            pl.BlockSpec((1, block, width), lead),
            pl.BlockSpec((1, block, width), lead),
            pl.BlockSpec((rank, width), lambda i: (0, 0)),
        ]
        + [ANY] * len(after),
        out_specs=[
            VMEM,
            VMEM,
            pl.BlockSpec((rank // 2, block), lambda i: (0, i)),
            pl.BlockSpec((rank // 2, block), lambda i: (0, i)),
        ],
        out_shape=[
            pltpu.VMEM((rows, width), jnp.float32),
            pltpu.VMEM((rows, width), jnp.float32),
            jax.ShapeDtypeStruct((rank // 2, rows), jnp.float32),
            jax.ShapeDtypeStruct((rank // 2, rows), jnp.float32),
        ],
        scratch_shapes=[pltpu.VMEM((3 * rank, width), jnp.bfloat16)],
        compiler_params=pltpu.CompilerParams(vmem_limit_bytes=26 * MIB),
        name="left",
    )(core, in_hbm(weights), in_hbm(copies), in_hbm(error), in_hbm(warm), *after)


def right_kernel(scale, block, core, mine, other, corrected, *refs):
    away, kept, left = refs[-3:]
    half, rows = mine.shape
    width = corrected.shape[1]
    first = core[0] == 0
    whole = ordered(first, mine[...] * scale, other[...] * scale)
    left[...] = whole
    parts = jnp.concatenate(split3(whole), axis=0)
    total = None
    for i in range(rows // block):
        cut = slice(i * block, (i + 1) * block)
        term = stacked_product(parts[:, cut], corrected[cut, :], ((1,), (0,)))
        total = term if total is None else total + term
    square = stacked_product(parts, whole, ((1,), (1,)))
    top, bottom = total[:half], total[half:]
    away_value, kept_value = jnp.where(first, bottom, top), jnp.where(first, top, bottom)
    gram = jnp.concatenate([square[:half], square[half:]], axis=1)
    if len(refs) > 3:
        away_before, kept_before = refs[:2]
        away_value = away_value + away_before[:, :width]
        kept_value = kept_value + kept_before[:, :width]
        gram = gram + kept_before[:, width:]
    away[:, :width] = away_value
    away[:, width:] = jnp.zeros_like(gram)
    kept[:, :width] = kept_value
    kept[:, width:] = gram


def right_call(core, mine, other, corrected, before, scale, block):
    half, rows = mine.shape
    width = corrected.shape[1]
    message = jax.ShapeDtypeStruct((half, width + 4 * half), jnp.float32)
    return pl.pallas_call(
        functools.partial(right_kernel, scale, block),
        in_specs=[SMEM] + [VMEM] * (3 + len(before)),
        out_specs=[VMEM] * 3,
        out_shape=[message, message, jax.ShapeDtypeStruct((2 * half, rows), jnp.float32)],
        compiler_params=pltpu.CompilerParams(vmem_limit_bytes=12 * MIB),
        name="right",
    )(core, mine, other, in_vmem(corrected), *before)


def factor_kernel(width, message, *refs):
    chunks = (len(refs) - 1) // 2
    left, inverse, basis = refs[:chunks], refs[chunks], refs[chunks + 1 :]
    half = message.shape[0]
    rank = 2 * half
    pair = message[:, width:]
    gram = jnp.concatenate([pair[:, :rank], pair[:, rank:]], axis=0)
    eye = jnp.where(
        lax.broadcasted_iota(jnp.int32, (rank, rank), 0) == lax.broadcasted_iota(jnp.int32, (rank, rank), 1), 1.0, 0.0
    )
    both = jnp.concatenate([gram, eye], axis=1)
    bands = [both[i : i + 8, :] for i in range(0, rank, 8)]
    group = 4
    for j in range(0, rank, group):
        band, line = divmod(j, 8)
        columns = [
            [jnp.broadcast_to(rest[:, j + k : j + k + 1], rest.shape) for k in range(group)] for rest in bands[band:]
        ]
        rows = [bands[band][line + k : line + k + 1, :] for k in range(group)]
        corner = [[columns[0][m][line + k : line + k + 1, :] for m in range(group)] for k in range(group)]
        roots, factors = [], []
        for k in range(group):
            root = lax.rsqrt(corner[k][k])
            rows[k] = rows[k] * root
            inverse[j + k : j + k + 1, :] = rows[k][:, rank:]
            factor = {m: corner[m][k] * root for m in range(k + 1, group)}
            for m in range(k + 1, group):
                rows[m] = rows[m] - factor[m] * rows[k]
                for n in range(k + 1, m + 1):
                    corner[m][n] = corner[m][n] - factor[m] * factor[n]
            roots.append(root)
            factors.append(factor)
        for k in reversed(range(group)):
            for m in range(k + 1, group):
                rows[k] = rows[k] - factors[k][m] * rows[m]
            rows[k] = rows[k] * roots[k]
        for i in range(band, rank // 8):
            column = columns[i - band]
            bands[i] = bands[i] - (
                (column[0] * rows[0] + column[1] * rows[1]) + (column[2] * rows[2] + column[3] * rows[3])
            )
    for chunk in range(chunks):
        rows = lax.dot_general(
            inverse[...],
            left[chunk][...],
            (((1,), (0,)), ((), ())),
            precision=lax.Precision.HIGHEST,
            preferred_element_type=jnp.float32,
        )
        high, middle, low = split3(rows.T)
        basis[chunk][...] = jnp.concatenate([high, high, middle, high, low, middle], axis=1)


def factor_call(message, left, width):
    half = message.shape[0]
    rank = 2 * half
    return pl.pallas_call(
        functools.partial(factor_kernel, width),
        in_specs=[VMEM] * (1 + len(left)),
        out_specs=[VMEM] * (1 + len(left)),
        out_shape=[jax.ShapeDtypeStruct((rank, rank), jnp.float32)]
        + [jax.ShapeDtypeStruct((piece.shape[1], 6 * rank), jnp.bfloat16) for piece in left],
        compiler_params=pltpu.CompilerParams(vmem_limit_bytes=12 * MIB),
        name="factor",
    )(message, *left)


def final_kernel(scale, chunks, core, mine, other, inverse, moment, *refs):
    weights, corrected, basis = refs[:chunks], refs[chunks : 2 * chunks], refs[2 * chunks : 3 * chunks]
    updated, velocity, carried, parts = refs[-4:]
    step = pl.program_id(0)
    rows, width = updated.shape
    here = pl.ds(pl.multiple_of(step * rows, rows), rows)

    @pl.when(step == 0)
    def _():
        whole = ordered(core[0] == 0, mine[:, :width] * scale, other[:, :width] * scale)
        right = lax.dot_general(
            inverse[...], whole, (((1,), (0,)), ((), ())), precision=lax.Precision.HIGHEST, preferred_element_type=jnp.float32
        )
        high, middle, low = split3(right)
        parts[...] = jnp.concatenate([high, middle, high, low, high, middle], axis=0)

    def work(chunk, at):
        there = pl.ds(pl.multiple_of(at, rows), rows)
        change = jnp.dot(basis[chunk][there, :], parts[...], preferred_element_type=jnp.float32)
        carried[0] = corrected[chunk][there, :] - change
        new, speed = nesterov(weights[chunk][there, :], change, moment[here, :])
        updated[...] = new
        velocity[...] = speed

    first = 0
    for chunk in range(chunks):
        count = corrected[chunk].shape[0] // rows
        here_now = jnp.logical_and(step >= first, step < first + count)
        pl.when(here_now)(functools.partial(work, chunk, (step - first) * rows))
        first += count


def final_call(core, mine, other, inverse, moment, weights, corrected, basis, after, scale, block):
    rows, width = moment.shape
    rank = inverse.shape[0]
    chunks = len(corrected)
    out = pl.BlockSpec((block, width), lambda i: (i, 0))
    large = [in_vmem(value) for value in (moment, *weights, *corrected, *basis)]
    return pl.pallas_call(
        functools.partial(final_kernel, scale, chunks),
        grid=(rows // block,),
        in_specs=[SMEM] + [VMEM] * (3 + len(large)) + [ANY] * len(after),
        out_specs=[out, out, pl.BlockSpec((1, block, width), lambda i: (0, i, 0))],
        out_shape=[
            jax.ShapeDtypeStruct((rows, width), jnp.float32),
            jax.ShapeDtypeStruct((rows, width), jnp.float32),
            jax.ShapeDtypeStruct((1, rows, width), jnp.float32),
        ],
        scratch_shapes=[pltpu.VMEM((6 * rank, width), jnp.bfloat16)],
        compiler_params=pltpu.CompilerParams(vmem_limit_bytes=16 * MIB),
        name="final",
    )(core, mine, other, inverse, *large, *after)


def sum_kernel(one, two, *refs):
    refs[-1][...] = one[...] + two[...]


def sum_call(one, two, after):
    return pl.pallas_call(
        sum_kernel,
        in_specs=[VMEM] * 2 + [ANY] * len(after),
        out_specs=VMEM,
        out_shape=jax.ShapeDtypeStruct(one.shape, one.dtype),
        compiler_params=pltpu.CompilerParams(vmem_limit_bytes=8 * MIB),
        name="sum",
    )(one, two, *after)


def away_kernel(core, weights, copies, *refs):
    at = 1 - core[0]
    refs[-1][...] = weights[at] - copies[0, at]


def term_kernel(core, weights, copies, received, *refs):
    at = core[0]
    refs[-1][...] = (weights[at] - copies[0, at]) + received[...]


def both_kernel(core, weights, copies, received, *refs):
    at = core[0]
    refs[-1][...] = (weights[at] - copies[0, at]) + (weights[at] - received[0, at])


def difference_call(kernel, core, operands, after):
    return pl.pallas_call(
        kernel,
        in_specs=[SMEM] + [VMEM] * len(operands) + [ANY] * len(after),
        out_specs=VMEM,
        out_shape=jax.ShapeDtypeStruct(operands[0].shape[1:], jnp.float32),
        compiler_params=pltpu.CompilerParams(vmem_limit_bytes=12 * MIB),
        name=kernel.__name__[:-7],
    )(core, *operands, *after)


def layer_kernel(scale, core, mine, other, weights, moment, *refs):
    updated, velocity, mark = refs[-3:]
    for value, at in ((mine, core[0]), (other, 1 - core[0])):
        updated[at], velocity[at] = nesterov(weights[at], value[...] * scale, moment[at])
    mark[...] = jnp.zeros_like(mark)


def layer_call(core, mine, other, weights, moment, after, scale):
    return pl.pallas_call(
        functools.partial(layer_kernel, scale),
        in_specs=[SMEM] + [VMEM] * 4 + [ANY] * len(after),
        out_specs=[VMEM] * 3,
        out_shape=[jax.ShapeDtypeStruct(weights.shape, jnp.float32)] * 2 + [jax.ShapeDtypeStruct((8, 128), jnp.float32)],
        compiler_params=pltpu.CompilerParams(vmem_limit_bytes=16 * MIB),
        name="layer",
    )(core, mine, other, weights, moment, *after)


def local(
    square_weights,
    square_copies,
    square_moment,
    broad_weights,
    broad_copies,
    broad_moment,
    embed_weights,
    embed_copies,
    embed_moment,
    embed_error,
    warm_start,
):
    replicas = lax.axis_size("replica")
    scale = 1 / replicas
    rank, width = warm_start.shape
    rows = embed_weights.shape[0]
    sizes = (rows // 4, rows - rows // 4) if rows % 2048 == 0 else (rows,)
    chunks = len(sizes)
    core = jnp.reshape(lax.axis_index("replica") % 2, (1,)).astype(jnp.int32)

    square_received = swap(square_copies, "replica", 1)
    corrected, held, left, after, before = [], [], [], (), ()
    start, exchanged = 0, []
    for chunk, size in enumerate(sizes):
        value, weights, away, kept = left_call(
            core, embed_weights, embed_copies, embed_error, warm_start, after, start, size, math.gcd(size, 256 << chunk)
        )
        start += size
        corrected.append(value)
        held.append(weights)
        half = sum_call(kept, swap(away, "replica", 1), exchanged)
        if chunk == 0:
            square_half = difference_call(
                both_kernel, core, (square_weights, square_copies, square_received), (away,)
            )
            after = (half, square_half)
            square_half_first = square_half
            square_half = sum_over_chips(square_half, ())
            exchanged.append(square_half)
            broad_away = difference_call(away_kernel, core, (broad_weights, broad_copies), (square_half_first,))
            broad_received = swap(broad_away, "replica", 1)
        half = sum_over_chips(half, ())
        exchanged.append(half)
        other = swap(half, "replica", 1)
        left.append((half, other))
    broad_half = difference_call(term_kernel, core, (broad_weights, broad_copies, broad_received), (half,))
    for chunk, size in enumerate(sizes):
        *before, left[chunk] = right_call(
            core, *left[chunk], corrected[chunk], before, scale, math.gcd(size, 256)
        )
    away, kept = before

    message = sum_call(kept, swap(away, "replica", 1), ())
    inner = lax.axis_size("inner")
    bit = 1
    square_other = swap(square_half, "replica", 1)
    while bit < inner:
        received = swap(message, "inner", bit)
        after = ()
        if 2 * bit >= inner:
            square_updated, square_velocity, mark = layer_call(
                core, square_half, square_other, square_weights, square_moment, (message,), scale
            )
            after = (mark,)
        message = sum_call(message, received, after)
        bit *= 2
    inverse, *basis = factor_call(message, left, width)
    right_half = sum_over_chips(message, (inverse,))
    broad_half = sum_over_chips(broad_half, (message,))
    broad_other = swap(broad_half, "replica", 1)
    broad_updated, broad_velocity, mark = layer_call(
        core, broad_half, broad_other, broad_weights, broad_moment, (right_half,), scale
    )
    right_other = swap(right_half, "replica", 1)
    embed_updated, embed_velocity, embed_carried = final_call(
        core, right_half, right_other, inverse, embed_moment, held, corrected, basis, (mark,), scale, math.gcd(rows, 256)
    )
    return (
        square_updated,
        square_velocity,
        broad_updated,
        broad_velocity,
        embed_updated,
        embed_velocity,
        embed_carried,
    )


def solution(mesh):
    in_specs = (
        P(None, "inner", None),
        P("replica", None, "inner", None),
        P(None, "inner", None),
        P(None, "inner", None),
        P("replica", None, "inner", None),
        P(None, "inner", None),
        P("inner", None),
        P("replica", "inner", None),
        P("inner", None),
        P("replica", "inner", None),
        P(),
    )
    out_specs = (
        P(None, "inner", None),
        P(None, "inner", None),
        P(None, "inner", None),
        P(None, "inner", None),
        P("inner", None),
        P("inner", None),
        P("replica", "inner", None),
    )
    return jax.shard_map(local, mesh=mesh, in_specs=in_specs, out_specs=out_specs, check_vma=False)
```

```python
import functools
import math

import jax
import jax.numpy as jnp
from jax import lax
from jax.experimental import pallas as pl
from jax.experimental.pallas import tpu as pltpu
from jax.sharding import PartitionSpec as P

outer_rate = 0.7
momentum_decay = 0.9
MIB = 1 << 20


def nesterov(weights, gradient, moment):
    velocity = momentum_decay * moment + gradient
    return (weights - outer_rate * (gradient + momentum_decay * velocity), velocity)


def split3(value):
    high = value.astype(jnp.bfloat16)
    rest = value - high.astype(jnp.float32)
    middle = rest.astype(jnp.bfloat16)
    low = (rest - middle.astype(jnp.float32)).astype(jnp.bfloat16)
    return high, middle, low


def stacked_product(parts, right, dims):
    rows = parts.shape[0] // 3
    high, middle, low = split3(right)
    dot = functools.partial(lax.dot_general, dimension_numbers=(dims, ((), ())), preferred_element_type=jnp.float32)
    one = dot(parts, high)
    two = dot(parts[: 2 * rows], middle)
    three = dot(parts[:rows], low)
    small = one[2 * rows :] + two[rows:] + three
    return one[:rows] + (one[rows : 2 * rows] + two[:rows] + small)


def swap(value, axis, bit):
    return lax.ppermute(value, axis, [(i, i ^ bit) for i in range(lax.axis_size(axis))])


def doubled(value, axis, first=1):
    bit = first
    while bit < lax.axis_size(axis):
        value = value + swap(value, axis, bit)
        bit *= 2
    return value


def sum_over_chips(value, after):
    bit = 2
    while bit < lax.axis_size("replica"):
        value = sum_call(value, swap(value, "replica", bit), after)
        bit *= 2
    return value


def in_hbm(value):
    return pltpu.with_memory_space_constraint(value, pltpu.HBM)


def in_vmem(value):
    return pltpu.with_memory_space_constraint(value, pltpu.VMEM)


VMEM = pl.BlockSpec(memory_space=pltpu.VMEM)
SMEM = pl.BlockSpec(memory_space=pltpu.SMEM)
ANY = pl.BlockSpec(memory_space=pl.ANY)


def ordered(first, mine, other):
    return jnp.concatenate([jnp.where(first, mine, other), jnp.where(first, other, mine)], axis=0)


def left_kernel(chunk_after, core, weights, copies, error, warm, *refs):
    corrected, held, away, kept, parts = refs[chunk_after:]
    step = pl.program_id(0)
    rows = weights.shape[0]
    half = away.shape[0]

    @pl.when(step == 0)
    def _():
        first = core[0] == 0
        top, bottom = warm[:half], warm[half:]
        both = jnp.concatenate([jnp.where(first, bottom, top), jnp.where(first, top, bottom)], axis=0)
        parts[...] = jnp.concatenate(split3(both), axis=0)

    value = weights[...] - copies[0] + error[0]
    here = pl.ds(pl.multiple_of(step * rows, rows), rows)
    corrected[here, :] = value
    held[here, :] = weights[...]
    left = stacked_product(parts[...], value, ((1,), (1,)))
    away[...] = left[:half]
    kept[...] = left[half:]


def left_call(core, weights, copies, error, warm, after, start, rows, block):
    rank, width = warm.shape
    first = start // block
    row = lambda i: (first + i, 0)
    lead = lambda i: (0, first + i, 0)
    return pl.pallas_call(
        functools.partial(left_kernel, len(after)),
        grid=(rows // block,),
        in_specs=[
            SMEM,
            pl.BlockSpec((block, width), row),
            pl.BlockSpec((1, block, width), lead),
            pl.BlockSpec((1, block, width), lead),
            pl.BlockSpec((rank, width), lambda i: (0, 0)),
        ]
        + [ANY] * len(after),
        out_specs=[
            VMEM,
            VMEM,
            pl.BlockSpec((rank // 2, block), lambda i: (0, i)),
            pl.BlockSpec((rank // 2, block), lambda i: (0, i)),
        ],
        out_shape=[
            pltpu.VMEM((rows, width), jnp.float32),
            pltpu.VMEM((rows, width), jnp.float32),
            jax.ShapeDtypeStruct((rank // 2, rows), jnp.float32),
            jax.ShapeDtypeStruct((rank // 2, rows), jnp.float32),
        ],
        scratch_shapes=[pltpu.VMEM((3 * rank, width), jnp.bfloat16)],
        compiler_params=pltpu.CompilerParams(vmem_limit_bytes=26 * MIB),
        name="left",
    )(core, in_hbm(weights), in_hbm(copies), in_hbm(error), in_hbm(warm), *after)


def right_kernel(scale, block, chunk, core, mine, other, corrected, *refs):
    away, kept, left = refs[-3:]
    half, rows = mine.shape
    width = corrected.shape[1]
    first = core[0] == 0
    whole = ordered(first, mine[...] * scale, other[...] * scale)
    left[...] = whole
    parts = jnp.concatenate(split3(whole), axis=0)
    total = None
    for i in range(rows // block):
        cut = slice(i * block, (i + 1) * block)
        here = slice(chunk * rows + i * block, chunk * rows + (i + 1) * block)
        term = stacked_product(parts[:, cut], corrected[here, :], ((1,), (0,)))
        total = term if total is None else total + term
    square = stacked_product(parts, whole, ((1,), (1,)))
    top, bottom = total[:half], total[half:]
    away_value, kept_value = jnp.where(first, bottom, top), jnp.where(first, top, bottom)
    gram = jnp.concatenate([square[:half], square[half:]], axis=1)
    if len(refs) > 3:
        away_before, kept_before = refs[:2]
        away_value = away_value + away_before[:, :width]
        kept_value = kept_value + kept_before[:, :width]
        gram = gram + kept_before[:, width:]
    away[:, :width] = away_value
    away[:, width:] = jnp.zeros_like(gram)
    kept[:, :width] = kept_value
    kept[:, width:] = gram


def right_call(core, mine, other, corrected, before, scale, block, chunk):
    half, rows = mine.shape
    width = corrected.shape[1]
    message = jax.ShapeDtypeStruct((half, width + 4 * half), jnp.float32)
    return pl.pallas_call(
        functools.partial(right_kernel, scale, block, chunk),
        in_specs=[SMEM] + [VMEM] * (3 + len(before)),
        out_specs=[VMEM] * 3,
        out_shape=[message, message, jax.ShapeDtypeStruct((2 * half, rows), jnp.float32)],
        compiler_params=pltpu.CompilerParams(vmem_limit_bytes=12 * MIB),
        name="right",
    )(core, mine, other, in_vmem(corrected), *before)


def factor_kernel(width, message, *refs):
    chunks = (len(refs) - 1) // 2
    left, inverse, basis = refs[:chunks], refs[chunks], refs[chunks + 1 :]
    half = message.shape[0]
    rank = 2 * half
    pair = message[:, width:]
    gram = jnp.concatenate([pair[:, :rank], pair[:, rank:]], axis=0)
    eye = jnp.where(
        lax.broadcasted_iota(jnp.int32, (rank, rank), 0) == lax.broadcasted_iota(jnp.int32, (rank, rank), 1), 1.0, 0.0
    )
    both = jnp.concatenate([gram, eye], axis=1)
    bands = [both[i : i + 8, :] for i in range(0, rank, 8)]
    group = 4
    for j in range(0, rank, group):
        band, line = divmod(j, 8)
        columns = [
            [jnp.broadcast_to(rest[:, j + k : j + k + 1], rest.shape) for k in range(group)] for rest in bands[band:]
        ]
        rows = [bands[band][line + k : line + k + 1, :] for k in range(group)]
        corner = [[columns[0][m][line + k : line + k + 1, :] for m in range(group)] for k in range(group)]
        roots, factors = [], []
        for k in range(group):
            root = lax.rsqrt(corner[k][k])
            rows[k] = rows[k] * root
            inverse[j + k : j + k + 1, :] = rows[k][:, rank:]
            factor = {m: corner[m][k] * root for m in range(k + 1, group)}
            for m in range(k + 1, group):
                rows[m] = rows[m] - factor[m] * rows[k]
                for n in range(k + 1, m + 1):
                    corner[m][n] = corner[m][n] - factor[m] * factor[n]
            roots.append(root)
            factors.append(factor)
        for k in reversed(range(group)):
            for m in range(k + 1, group):
                rows[k] = rows[k] - factors[k][m] * rows[m]
            rows[k] = rows[k] * roots[k]
        for i in range(band, rank // 8):
            column = columns[i - band]
            bands[i] = bands[i] - (
                (column[0] * rows[0] + column[1] * rows[1]) + (column[2] * rows[2] + column[3] * rows[3])
            )
    for chunk in range(chunks):
        rows = lax.dot_general(
            inverse[...],
            left[chunk][...],
            (((1,), (0,)), ((), ())),
            precision=lax.Precision.HIGHEST,
            preferred_element_type=jnp.float32,
        )
        high, middle, low = split3(rows.T)
        basis[chunk][...] = jnp.concatenate([high, high, middle, high, low, middle], axis=1)


def factor_call(message, left, width):
    half = message.shape[0]
    rank = 2 * half
    return pl.pallas_call(
        functools.partial(factor_kernel, width),
        in_specs=[VMEM] * (1 + len(left)),
        out_specs=[VMEM] * (1 + len(left)),
        out_shape=[jax.ShapeDtypeStruct((rank, rank), jnp.float32)]
        + [jax.ShapeDtypeStruct((piece.shape[1], 6 * rank), jnp.bfloat16) for piece in left],
        compiler_params=pltpu.CompilerParams(vmem_limit_bytes=12 * MIB),
        name="factor",
    )(message, *left)


def final_kernel(scale, chunks, core, mine, other, inverse, moment, weights, corrected, *refs):
    basis = refs[:chunks]
    updated, velocity, carried, parts = refs[-4:]
    step = pl.program_id(0)
    rows, width = updated.shape
    here = pl.ds(pl.multiple_of(step * rows, rows), rows)

    @pl.when(step == 0)
    def _():
        whole = ordered(core[0] == 0, mine[:, :width] * scale, other[:, :width] * scale)
        right = lax.dot_general(
            inverse[...], whole, (((1,), (0,)), ((), ())), precision=lax.Precision.HIGHEST, preferred_element_type=jnp.float32
        )
        high, middle, low = split3(right)
        parts[...] = jnp.concatenate([high, middle, high, low, high, middle], axis=0)

    def work(chunk, at):
        there = pl.ds(pl.multiple_of(at, rows), rows)
        change = jnp.dot(basis[chunk][there, :], parts[...], preferred_element_type=jnp.float32)
        carried[0] = corrected[here, :] - change
        new, speed = nesterov(weights[here, :], change, moment[here, :])
        updated[...] = new
        velocity[...] = speed

    first = 0
    for chunk in range(chunks):
        count = basis[chunk].shape[0] // rows
        here_now = jnp.logical_and(step >= first, step < first + count)
        pl.when(here_now)(functools.partial(work, chunk, (step - first) * rows))
        first += count


def final_call(core, mine, other, inverse, moment, weights, corrected, basis, after, scale, block):
    rows, width = moment.shape
    rank = inverse.shape[0]
    chunks = len(basis)
    out = pl.BlockSpec((block, width), lambda i: (i, 0))
    large = [in_vmem(value) for value in (moment, weights, corrected, *basis)]
    return pl.pallas_call(
        functools.partial(final_kernel, scale, chunks),
        grid=(rows // block,),
        in_specs=[SMEM] + [VMEM] * (3 + len(large)) + [ANY] * len(after),
        out_specs=[out, out, pl.BlockSpec((1, block, width), lambda i: (0, i, 0))],
        out_shape=[
            jax.ShapeDtypeStruct((rows, width), jnp.float32),
            jax.ShapeDtypeStruct((rows, width), jnp.float32),
            jax.ShapeDtypeStruct((1, rows, width), jnp.float32),
        ],
        scratch_shapes=[pltpu.VMEM((6 * rank, width), jnp.bfloat16)],
        compiler_params=pltpu.CompilerParams(vmem_limit_bytes=24 * MIB),
        name="final",
    )(core, mine, other, inverse, *large, *after)


def sum_kernel(parts, one, two, *refs):
    width = one.shape[1] // parts
    for i, out in enumerate(refs[len(refs) - parts :]):
        cut = slice(i * width, (i + 1) * width)
        out[...] = one[:, cut] + two[:, cut]


def sum_call(one, two, after, parts=1):
    out = jax.ShapeDtypeStruct((one.shape[0], one.shape[1] // parts), one.dtype)
    return pl.pallas_call(
        functools.partial(sum_kernel, parts),
        in_specs=[VMEM] * 2 + [ANY] * len(after),
        out_specs=VMEM if parts == 1 else [VMEM] * parts,
        out_shape=out if parts == 1 else [out] * parts,
        compiler_params=pltpu.CompilerParams(vmem_limit_bytes=8 * MIB),
        name="sum",
    )(one, two, *after)


def away_kernel(core, weights, copies, *refs):
    refs[-1][...] = weights[0] - copies[0, 0]


def both_kernel(core, weights, copies, received, *refs):
    refs[-1][...] = (weights[0] - copies[0, 0]) + (weights[0] - received[0, 0])


def half_call(kernel, flip, core, weights, copies, after):
    _, rows, width = weights.shape
    block = rows // 2 if rows % 16 == 0 else rows
    pick = (lambda core: 1 - core[0]) if flip else (lambda core: core[0])
    part = pl.BlockSpec((1, block, width), lambda i, core: (pick(core), i, 0))
    whole = pl.BlockSpec((1, 1, block, width), lambda i, core: (0, pick(core), i, 0))
    return pl.pallas_call(
        kernel,
        grid_spec=pltpu.PrefetchScalarGridSpec(
            num_scalar_prefetch=1,
            grid=(rows // block,),
            in_specs=[part] + [whole] * len(copies) + [ANY] * len(after),
            out_specs=pl.BlockSpec((block, width), lambda i, core: (i, 0)),
        ),
        out_shape=jax.ShapeDtypeStruct((rows, width), jnp.float32),
        compiler_params=pltpu.CompilerParams(vmem_limit_bytes=12 * MIB),
        name=kernel.__name__[:-7],
    )(core, in_hbm(weights), in_hbm(copies[0]), *copies[1:], *after)


def term_kernel(core, weights, copies, received, *refs):
    at = core[0]
    refs[-1][...] = (weights[at] - copies[0, at]) + received[...]


def term_call(core, weights, copies, received, after):
    return pl.pallas_call(
        term_kernel,
        in_specs=[SMEM] + [VMEM] * 3 + [ANY] * len(after),
        out_specs=VMEM,
        out_shape=jax.ShapeDtypeStruct(weights.shape[1:], jnp.float32),
        compiler_params=pltpu.CompilerParams(vmem_limit_bytes=12 * MIB),
        name="term",
    )(core, weights, copies, received, *after)


def layer_kernel(scale, core, mine, other, weights, moment, *refs):
    updated, velocity, mark = refs[-3:]
    for value, at in ((mine, core[0]), (other, 1 - core[0])):
        updated[at], velocity[at] = nesterov(weights[at], value[...] * scale, moment[at])
    mark[...] = jnp.zeros_like(mark)


def layer_call(core, mine, other, weights, moment, after, scale):
    return pl.pallas_call(
        functools.partial(layer_kernel, scale),
        in_specs=[SMEM] + [VMEM] * 4 + [ANY] * len(after),
        out_specs=[VMEM] * 3,
        out_shape=[jax.ShapeDtypeStruct(weights.shape, jnp.float32)] * 2 + [jax.ShapeDtypeStruct((8, 128), jnp.float32)],
        compiler_params=pltpu.CompilerParams(vmem_limit_bytes=16 * MIB),
        name="layer",
    )(core, mine, other, weights, moment, *after)


def local(
    square_weights,
    square_copies,
    square_moment,
    broad_weights,
    broad_copies,
    broad_moment,
    embed_weights,
    embed_copies,
    embed_moment,
    embed_error,
    warm_start,
):
    replicas = lax.axis_size("replica")
    scale = 1 / replicas
    rank, width = warm_start.shape
    rows = embed_weights.shape[0]
    core = jnp.reshape(lax.axis_index("replica") % 2, (1,)).astype(jnp.int32)

    square_received = swap(square_copies, "replica", 1)
    broad_away = half_call(away_kernel, True, core, broad_weights, (broad_copies,), ())
    square_half = half_call(both_kernel, False, core, square_weights, (square_copies, square_received), (broad_away,))
    broad_received = swap(broad_away, "replica", 1)
    chunks = 2 if rows % 512 == 0 else 1
    corrected, held, away, kept = left_call(
        core, embed_weights, embed_copies, embed_error, warm_start, (square_half,), 0, rows, math.gcd(rows, 512)
    )
    square_half = sum_over_chips(square_half, ())
    pair = sum_call(kept, swap(away, "replica", 1), (square_half,), chunks)
    halves, others, ready = [], [], ()
    for piece in pair if chunks > 1 else [pair]:
        halves.append(sum_over_chips(piece, ready))
        others.append(swap(halves[-1], "replica", 1))
        ready = (others[-1],)
    broad_half = term_call(core, broad_weights, broad_copies, broad_received, tuple(halves))
    before, left = [], []
    for chunk, half in enumerate(halves):
        *before, piece = right_call(
            core, half, others[chunk], corrected, before, scale, math.gcd(rows // chunks, 256), chunk
        )
        left.append(piece)
    away, kept = before

    message = sum_call(kept, swap(away, "replica", 1), ())
    inner = lax.axis_size("inner")
    bit = 1
    square_other = swap(square_half, "replica", 1)
    while bit < inner:
        received = swap(message, "inner", bit)
        after = ()
        if 2 * bit >= inner:
            square_updated, square_velocity, mark = layer_call(
                core, square_half, square_other, square_weights, square_moment, (message,), scale
            )
            after = (mark,)
        message = sum_call(message, received, after)
        bit *= 2
    inverse, *basis = factor_call(message, left, width)
    right_half = sum_over_chips(message, (inverse,))
    broad_half = sum_over_chips(broad_half, (message,))
    broad_other = swap(broad_half, "replica", 1)
    broad_updated, broad_velocity, mark = layer_call(
        core, broad_half, broad_other, broad_weights, broad_moment, (right_half,), scale
    )
    right_other = swap(right_half, "replica", 1)
    embed_updated, embed_velocity, embed_carried = final_call(
        core, right_half, right_other, inverse, embed_moment, held, corrected, basis, (mark,), scale, math.gcd(rows, 512)
    )
    return (
        square_updated,
        square_velocity,
        broad_updated,
        broad_velocity,
        embed_updated,
        embed_velocity,
        embed_carried,
    )


def solution(mesh):
    in_specs = (
        P(None, "inner", None),
        P("replica", None, "inner", None),
        P(None, "inner", None),
        P(None, "inner", None),
        P("replica", None, "inner", None),
        P(None, "inner", None),
        P("inner", None),
        P("replica", "inner", None),
        P("inner", None),
        P("replica", "inner", None),
        P(),
    )
    out_specs = (
        P(None, "inner", None),
        P(None, "inner", None),
        P(None, "inner", None),
        P(None, "inner", None),
        P("inner", None),
        P("inner", None),
        P("replica", "inner", None),
    )
    return jax.shard_map(local, mesh=mesh, in_specs=in_specs, out_specs=out_specs, check_vma=False)
```

```python
import functools
import math

import jax
import jax.numpy as jnp
from jax import lax
from jax.experimental import pallas as pl
from jax.experimental.pallas import tpu as pltpu
from jax.sharding import PartitionSpec as P

outer_rate = 0.7
momentum_decay = 0.9
MIB = 1 << 20


def nesterov(weights, gradient, moment):
    velocity = momentum_decay * moment + gradient
    return (weights - outer_rate * (gradient + momentum_decay * velocity), velocity)


def split3(value):
    high = value.astype(jnp.bfloat16)
    rest = value - high.astype(jnp.float32)
    middle = rest.astype(jnp.bfloat16)
    low = (rest - middle.astype(jnp.float32)).astype(jnp.bfloat16)
    return high, middle, low


def stacked_product(parts, right, dims):
    rows = parts.shape[0] // 3
    high, middle, low = split3(right)
    dot = functools.partial(lax.dot_general, dimension_numbers=(dims, ((), ())), preferred_element_type=jnp.float32)
    one = dot(parts, high)
    two = dot(parts[: 2 * rows], middle)
    three = dot(parts[:rows], low)
    small = one[2 * rows :] + two[rows:] + three
    return one[:rows] + (one[rows : 2 * rows] + two[:rows] + small)


def swap(value, axis, bit):
    return lax.ppermute(value, axis, [(i, i ^ bit) for i in range(lax.axis_size(axis))])


def doubled(value, axis, first=1):
    bit = first
    while bit < lax.axis_size(axis):
        value = value + swap(value, axis, bit)
        bit *= 2
    return value


def part_kernel(one, two, *refs):
    left, right = refs[-2:]
    width = left.shape[1]
    left[...] = one[:, :width] + two[:, :width]
    right[...] = one[:, width:] + two[:, width:]


def part_call(one, two, after, width):
    rows, total = one.shape
    return pl.pallas_call(
        part_kernel,
        in_specs=[VMEM] * 2 + [ANY] * len(after),
        out_specs=[VMEM] * 2,
        out_shape=[
            jax.ShapeDtypeStruct((rows, width), jnp.float32),
            jax.ShapeDtypeStruct((rows, total - width), jnp.float32),
        ],
        compiler_params=pltpu.CompilerParams(vmem_limit_bytes=8 * MIB),
        name="part",
    )(one, two, *after)


def sum_over_chips(value, after):
    bit = 2
    while bit < lax.axis_size("replica"):
        value = sum_call(value, swap(value, "replica", bit), after)
        bit *= 2
    return value


def in_hbm(value):
    return pltpu.with_memory_space_constraint(value, pltpu.HBM)


def in_vmem(value):
    return pltpu.with_memory_space_constraint(value, pltpu.VMEM)


VMEM = pl.BlockSpec(memory_space=pltpu.VMEM)
SMEM = pl.BlockSpec(memory_space=pltpu.SMEM)
ANY = pl.BlockSpec(memory_space=pl.ANY)


def ordered(first, mine, other):
    return jnp.concatenate([jnp.where(first, mine, other), jnp.where(first, other, mine)], axis=0)


def left_kernel(chunk_after, core, weights, copies, error, warm, *refs):
    corrected, away, kept, parts = refs[chunk_after:]
    step = pl.program_id(0)
    rows = weights.shape[0]
    half = away.shape[0]

    @pl.when(step == 0)
    def _():
        first = core[0] == 0
        top, bottom = warm[:half], warm[half:]
        both = jnp.concatenate([jnp.where(first, bottom, top), jnp.where(first, top, bottom)], axis=0)
        parts[...] = jnp.concatenate(split3(both), axis=0)

    value = weights[...] - copies[0] + error[0]
    here = pl.ds(pl.multiple_of(step * rows, rows), rows)
    corrected[here, :] = value
    left = stacked_product(parts[...], value, ((1,), (1,)))
    away[...] = left[:half]
    kept[...] = left[half:]


def left_call(core, weights, copies, error, warm, after, start, rows, block):
    rank, width = warm.shape
    first = start // block
    row = lambda i: (first + i, 0)
    lead = lambda i: (0, first + i, 0)
    return pl.pallas_call(
        functools.partial(left_kernel, len(after)),
        grid=(rows // block,),
        in_specs=[
            SMEM,
            pl.BlockSpec((block, width), row),
            pl.BlockSpec((1, block, width), lead),
            pl.BlockSpec((1, block, width), lead),
            pl.BlockSpec((rank, width), lambda i: (0, 0)),
        ]
        + [ANY] * len(after),
        out_specs=[
            VMEM,
            pl.BlockSpec((rank // 2, block), lambda i: (0, i)),
            pl.BlockSpec((rank // 2, block), lambda i: (0, i)),
        ],
        out_shape=[
            pltpu.VMEM((rows, width), jnp.float32),
            jax.ShapeDtypeStruct((rank // 2, rows), jnp.float32),
            jax.ShapeDtypeStruct((rank // 2, rows), jnp.float32),
        ],
        scratch_shapes=[pltpu.VMEM((3 * rank, width), jnp.bfloat16)],
        compiler_params=pltpu.CompilerParams(vmem_limit_bytes=26 * MIB),
        name="left",
    )(core, in_hbm(weights), in_hbm(copies), in_hbm(error), in_hbm(warm), *after)


def right_kernel(scale, block, chunk, core, mine, other, corrected, *refs):
    away, kept, left = refs[-3:]
    half, rows = mine.shape
    width = corrected.shape[1]
    first = core[0] == 0
    whole = ordered(first, mine[...] * scale, other[...] * scale)
    left[...] = whole
    parts = jnp.concatenate(split3(whole), axis=0)
    total = None
    for i in range(rows // block):
        cut = slice(i * block, (i + 1) * block)
        here = slice(chunk * rows + i * block, chunk * rows + (i + 1) * block)
        term = stacked_product(parts[:, cut], corrected[here, :], ((1,), (0,)))
        total = term if total is None else total + term
    square = stacked_product(parts, whole, ((1,), (1,)))
    top, bottom = total[:half], total[half:]
    away_value, kept_value = jnp.where(first, bottom, top), jnp.where(first, top, bottom)
    gram = jnp.concatenate([square[:half], square[half:]], axis=1)
    if len(refs) > 3:
        away_before, kept_before = refs[:2]
        away_value = away_value + away_before[:, :width]
        kept_value = kept_value + kept_before[:, :width]
        gram = gram + kept_before[:, width:]
    away[:, :width] = away_value
    away[:, width:] = jnp.zeros_like(gram)
    kept[:, :width] = kept_value
    kept[:, width:] = gram


def right_call(core, mine, other, corrected, before, scale, block, chunk):
    half, rows = mine.shape
    width = corrected.shape[1]
    message = jax.ShapeDtypeStruct((half, width + 4 * half), jnp.float32)
    return pl.pallas_call(
        functools.partial(right_kernel, scale, block, chunk),
        in_specs=[SMEM] + [VMEM] * (3 + len(before)),
        out_specs=[VMEM] * 3,
        out_shape=[message, message, jax.ShapeDtypeStruct((2 * half, rows), jnp.float32)],
        compiler_params=pltpu.CompilerParams(vmem_limit_bytes=12 * MIB),
        name="right",
    )(core, mine, other, in_vmem(corrected), *before)


def factor_kernel(message, *refs):
    chunks = (len(refs) - 1) // 2
    left, inverse, basis = refs[:chunks], refs[chunks], refs[chunks + 1 :]
    half = message.shape[0]
    rank = 2 * half
    pair = message[...]
    gram = jnp.concatenate([pair[:, :rank], pair[:, rank:]], axis=0)
    eye = jnp.where(
        lax.broadcasted_iota(jnp.int32, (rank, rank), 0) == lax.broadcasted_iota(jnp.int32, (rank, rank), 1), 1.0, 0.0
    )
    both = jnp.concatenate([gram, eye], axis=1)
    bands = [both[i : i + 8, :] for i in range(0, rank, 8)]
    group = 4
    for j in range(0, rank, group):
        band, line = divmod(j, 8)
        columns = [
            [jnp.broadcast_to(rest[:, j + k : j + k + 1], rest.shape) for k in range(group)] for rest in bands[band:]
        ]
        rows = [bands[band][line + k : line + k + 1, :] for k in range(group)]
        corner = [[columns[0][m][line + k : line + k + 1, :] for m in range(group)] for k in range(group)]
        roots, factors = [], []
        for k in range(group):
            root = lax.rsqrt(corner[k][k])
            rows[k] = rows[k] * root
            inverse[j + k : j + k + 1, :] = rows[k][:, rank:]
            factor = {m: corner[m][k] * root for m in range(k + 1, group)}
            for m in range(k + 1, group):
                rows[m] = rows[m] - factor[m] * rows[k]
                for n in range(k + 1, m + 1):
                    corner[m][n] = corner[m][n] - factor[m] * factor[n]
            roots.append(root)
            factors.append(factor)
        for k in reversed(range(group)):
            for m in range(k + 1, group):
                rows[k] = rows[k] - factors[k][m] * rows[m]
            rows[k] = rows[k] * roots[k]
        for i in range(band, rank // 8):
            column = columns[i - band]
            bands[i] = bands[i] - (
                (column[0] * rows[0] + column[1] * rows[1]) + (column[2] * rows[2] + column[3] * rows[3])
            )
    for chunk in range(chunks):
        rows = lax.dot_general(
            inverse[...],
            left[chunk][...],
            (((1,), (0,)), ((), ())),
            precision=lax.Precision.HIGHEST,
            preferred_element_type=jnp.float32,
        )
        high, middle, low = split3(rows.T)
        basis[chunk][...] = jnp.concatenate([high, high, middle, high, low, middle], axis=1)


def factor_call(message, left):
    half = message.shape[0]
    rank = 2 * half
    return pl.pallas_call(
        factor_kernel,
        in_specs=[VMEM] * (1 + len(left)),
        out_specs=[VMEM] * (1 + len(left)),
        out_shape=[jax.ShapeDtypeStruct((rank, rank), jnp.float32)]
        + [jax.ShapeDtypeStruct((piece.shape[1], 6 * rank), jnp.bfloat16) for piece in left],
        compiler_params=pltpu.CompilerParams(vmem_limit_bytes=12 * MIB),
        name="factor",
    )(message, *left)


def final_kernel(scale, chunks, core, mine, other, inverse, moment, weights, corrected, *refs):
    basis = refs[:chunks]
    updated, velocity, carried, parts = refs[-4:]
    step = pl.program_id(0)
    rows, width = updated.shape
    here = pl.ds(pl.multiple_of(step * rows, rows), rows)

    @pl.when(step == 0)
    def _():
        whole = ordered(core[0] == 0, mine[:, :width] * scale, other[:, :width] * scale)
        right = lax.dot_general(
            inverse[...], whole, (((1,), (0,)), ((), ())), precision=lax.Precision.HIGHEST, preferred_element_type=jnp.float32
        )
        high, middle, low = split3(right)
        parts[...] = jnp.concatenate([high, middle, high, low, high, middle], axis=0)

    def work(chunk, at):
        there = pl.ds(pl.multiple_of(at, rows), rows)
        change = jnp.dot(basis[chunk][there, :], parts[...], preferred_element_type=jnp.float32)
        carried[0] = corrected[here, :] - change
        new, speed = nesterov(weights[here, :], change, moment[here, :])
        updated[...] = new
        velocity[...] = speed

    first = 0
    for chunk in range(chunks):
        count = basis[chunk].shape[0] // rows
        here_now = jnp.logical_and(step >= first, step < first + count)
        pl.when(here_now)(functools.partial(work, chunk, (step - first) * rows))
        first += count


def final_call(core, mine, other, inverse, moment, weights, corrected, basis, after, scale, block):
    rows, width = moment.shape
    rank = inverse.shape[0]
    chunks = len(basis)
    out = pl.BlockSpec((block, width), lambda i: (i, 0))
    large = [in_vmem(value) for value in (moment, weights, corrected, *basis)]
    return pl.pallas_call(
        functools.partial(final_kernel, scale, chunks),
        grid=(rows // block,),
        in_specs=[SMEM] + [VMEM] * (3 + len(large)) + [ANY] * len(after),
        out_specs=[out, out, pl.BlockSpec((1, block, width), lambda i: (0, i, 0))],
        out_shape=[
            jax.ShapeDtypeStruct((rows, width), jnp.float32),
            jax.ShapeDtypeStruct((rows, width), jnp.float32),
            jax.ShapeDtypeStruct((1, rows, width), jnp.float32),
        ],
        scratch_shapes=[pltpu.VMEM((6 * rank, width), jnp.bfloat16)],
        compiler_params=pltpu.CompilerParams(vmem_limit_bytes=24 * MIB),
        name="final",
    )(core, mine, other, inverse, *large, *after)


def sum_kernel(parts, one, two, *refs):
    width = one.shape[1] // parts
    for i, out in enumerate(refs[len(refs) - parts :]):
        cut = slice(i * width, (i + 1) * width)
        out[...] = one[:, cut] + two[:, cut]


def sum_call(one, two, after, parts=1):
    out = jax.ShapeDtypeStruct((one.shape[0], one.shape[1] // parts), one.dtype)
    return pl.pallas_call(
        functools.partial(sum_kernel, parts),
        in_specs=[VMEM] * 2 + [ANY] * len(after),
        out_specs=VMEM if parts == 1 else [VMEM] * parts,
        out_shape=out if parts == 1 else [out] * parts,
        compiler_params=pltpu.CompilerParams(vmem_limit_bytes=8 * MIB),
        name="sum",
    )(one, two, *after)


def away_kernel(core, weights, copies, *refs):
    refs[-1][...] = weights[0] - copies[0, 0]


def both_kernel(core, weights, copies, received, *refs):
    refs[-1][...] = (weights[0] - copies[0, 0]) + (weights[0] - received[0, 0])


def half_call(kernel, flip, core, weights, copies, after):
    _, rows, width = weights.shape
    block = rows // 2 if rows % 16 == 0 else rows
    pick = (lambda core: 1 - core[0]) if flip else (lambda core: core[0])
    part = pl.BlockSpec((1, block, width), lambda i, core: (pick(core), i, 0))
    whole = pl.BlockSpec((1, 1, block, width), lambda i, core: (0, pick(core), i, 0))
    return pl.pallas_call(
        kernel,
        grid_spec=pltpu.PrefetchScalarGridSpec(
            num_scalar_prefetch=1,
            grid=(rows // block,),
            in_specs=[part] + [whole] * len(copies) + [ANY] * len(after),
            out_specs=pl.BlockSpec((block, width), lambda i, core: (i, 0)),
        ),
        out_shape=jax.ShapeDtypeStruct((rows, width), jnp.float32),
        compiler_params=pltpu.CompilerParams(vmem_limit_bytes=12 * MIB),
        name=kernel.__name__[:-7],
    )(core, in_hbm(weights), in_hbm(copies[0]), *copies[1:], *after)


def term_kernel(core, weights, copies, received, *refs):
    at = core[0]
    refs[-1][...] = (weights[at] - copies[0, at]) + received[...]


def term_call(core, weights, copies, received, after):
    return pl.pallas_call(
        term_kernel,
        in_specs=[SMEM] + [VMEM] * 3 + [ANY] * len(after),
        out_specs=VMEM,
        out_shape=jax.ShapeDtypeStruct(weights.shape[1:], jnp.float32),
        compiler_params=pltpu.CompilerParams(vmem_limit_bytes=12 * MIB),
        name="term",
    )(core, weights, copies, received, *after)


def layer_kernel(scale, core, mine, other, weights, moment, *refs):
    updated, velocity, mark = refs[-3:]
    for value, at in ((mine, core[0]), (other, 1 - core[0])):
        updated[at], velocity[at] = nesterov(weights[at], value[...] * scale, moment[at])
    mark[...] = jnp.zeros_like(mark)


def layer_call(core, mine, other, weights, moment, after, scale):
    return pl.pallas_call(
        functools.partial(layer_kernel, scale),
        in_specs=[SMEM] + [VMEM] * 4 + [ANY] * len(after),
        out_specs=[VMEM] * 3,
        out_shape=[jax.ShapeDtypeStruct(weights.shape, jnp.float32)] * 2 + [jax.ShapeDtypeStruct((8, 128), jnp.float32)],
        compiler_params=pltpu.CompilerParams(vmem_limit_bytes=16 * MIB),
        name="layer",
    )(core, mine, other, weights, moment, *after)


def local(
    square_weights,
    square_copies,
    square_moment,
    broad_weights,
    broad_copies,
    broad_moment,
    embed_weights,
    embed_copies,
    embed_moment,
    embed_error,
    warm_start,
):
    replicas = lax.axis_size("replica")
    scale = 1 / replicas
    rank, width = warm_start.shape
    rows = embed_weights.shape[0]
    core = jnp.reshape(lax.axis_index("replica") & 1, (1,)).astype(jnp.int32)

    square_received = swap(square_copies, "replica", 1)
    broad_away = half_call(away_kernel, True, core, broad_weights, (broad_copies,), ())
    square_half = half_call(both_kernel, False, core, square_weights, (square_copies, square_received), (broad_away,))
    broad_received = swap(broad_away, "replica", 1)
    chunks = 2 if rows % 512 == 0 else 1
    corrected, away, kept = left_call(
        core, embed_weights, embed_copies, embed_error, warm_start, (square_half,), 0, rows, math.gcd(rows, 512)
    )
    square_half = sum_over_chips(square_half, ())
    pair = sum_call(kept, swap(away, "replica", 1), (square_half,), chunks)
    halves, others, ready = [], [], ()
    for piece in pair if chunks > 1 else [pair]:
        halves.append(sum_over_chips(piece, ready))
        others.append(swap(halves[-1], "replica", 1))
        ready = (others[-1],)
    broad_half = term_call(core, broad_weights, broad_copies, broad_received, tuple(halves))
    before, left = [], []
    for chunk, half in enumerate(halves):
        *before, piece = right_call(
            core, half, others[chunk], corrected, before, scale, math.gcd(rows // chunks, 256), chunk
        )
        left.append(piece)
    away, kept = before

    message = sum_call(kept, swap(away, "replica", 1), ())
    inner = lax.axis_size("inner")
    bit = 1
    while 2 * bit < inner:
        message = sum_call(message, swap(message, "inner", bit), ())
        bit *= 2
    square_other = swap(square_half, "replica", 1)
    received = swap(message, "inner", bit)
    square_updated, square_velocity, mark = layer_call(
        core, square_half, square_other, square_weights, square_moment, (message,), scale
    )
    message, gram = part_call(message, received, (mark,), width)
    inverse, *basis = factor_call(gram, left)
    right_half = sum_over_chips(message, (inverse,))
    broad_half = sum_over_chips(broad_half, (message,))
    broad_other = swap(broad_half, "replica", 1)
    broad_updated, broad_velocity, mark = layer_call(
        core, broad_half, broad_other, broad_weights, broad_moment, (right_half,), scale
    )
    right_other = swap(right_half, "replica", 1)
    embed_updated, embed_velocity, embed_carried = final_call(
        core, right_half, right_other, inverse, embed_moment, embed_weights, corrected, basis, (mark,), scale, math.gcd(rows, 512)
    )
    return (
        square_updated,
        square_velocity,
        broad_updated,
        broad_velocity,
        embed_updated,
        embed_velocity,
        embed_carried,
    )


def solution(mesh):
    in_specs = (
        P(None, "inner", None),
        P("replica", None, "inner", None),
        P(None, "inner", None),
        P(None, "inner", None),
        P("replica", None, "inner", None),
        P(None, "inner", None),
        P("inner", None),
        P("replica", "inner", None),
        P("inner", None),
        P("replica", "inner", None),
        P(),
    )
    out_specs = (
        P(None, "inner", None),
        P(None, "inner", None),
        P(None, "inner", None),
        P(None, "inner", None),
        P("inner", None),
        P("inner", None),
        P("replica", "inner", None),
    )
    return jax.shard_map(local, mesh=mesh, in_specs=in_specs, out_specs=out_specs, check_vma=False)
```

```python
import functools
import math

import jax
import jax.numpy as jnp
from jax import lax
from jax.experimental import pallas as pl
from jax.experimental.pallas import tpu as pltpu
from jax.sharding import PartitionSpec as P

outer_rate = 0.7
momentum_decay = 0.9
MIB = 1 << 20


def nesterov(weights, gradient, moment):
    velocity = momentum_decay * moment + gradient
    return (weights - outer_rate * (gradient + momentum_decay * velocity), velocity)


def split3(value):
    high = value.astype(jnp.bfloat16)
    rest = value - high.astype(jnp.float32)
    middle = rest.astype(jnp.bfloat16)
    low = (rest - middle.astype(jnp.float32)).astype(jnp.bfloat16)
    return high, middle, low


def stacked_product(parts, right, dims):
    rows = parts.shape[0] // 3
    high, middle, low = split3(right)
    dot = functools.partial(lax.dot_general, dimension_numbers=(dims, ((), ())), preferred_element_type=jnp.float32)
    one = dot(parts, high)
    two = dot(parts[: 2 * rows], middle)
    three = dot(parts[:rows], low)
    small = one[2 * rows :] + two[rows:] + three
    return one[:rows] + (one[rows : 2 * rows] + two[:rows] + small)


def swap(value, axis, bit):
    return lax.ppermute(value, axis, [(i, i ^ bit) for i in range(lax.axis_size(axis))])


def doubled(value, axis, first=1):
    bit = first
    while bit < lax.axis_size(axis):
        value = value + swap(value, axis, bit)
        bit *= 2
    return value


def part_kernel(one, two, *refs):
    left, right = refs[-2:]
    width = left.shape[1]
    left[...] = one[:, :width] + two[:, :width]
    right[...] = one[:, width:] + two[:, width:]


def part_call(one, two, after, width):
    rows, total = one.shape
    return pl.pallas_call(
        part_kernel,
        in_specs=[VMEM] * 2 + [ANY] * len(after),
        out_specs=[VMEM] * 2,
        out_shape=[
            jax.ShapeDtypeStruct((rows, width), jnp.float32),
            jax.ShapeDtypeStruct((rows, total - width), jnp.float32),
        ],
        compiler_params=pltpu.CompilerParams(vmem_limit_bytes=8 * MIB),
        name="part",
    )(one, two, *after)


def sum_over_chips(value, after):
    bit = 2
    while bit < lax.axis_size("replica"):
        value = sum_call(value, swap(value, "replica", bit), after)
        bit *= 2
    return value


def in_hbm(value):
    return pltpu.with_memory_space_constraint(value, pltpu.HBM)


def in_vmem(value):
    return pltpu.with_memory_space_constraint(value, pltpu.VMEM)


VMEM = pl.BlockSpec(memory_space=pltpu.VMEM)
SMEM = pl.BlockSpec(memory_space=pltpu.SMEM)
ANY = pl.BlockSpec(memory_space=pl.ANY)


def ordered(first, mine, other):
    return jnp.concatenate([jnp.where(first, mine, other), jnp.where(first, other, mine)], axis=0)


def left_kernel(chunk_after, core, weights, copies, error, warm, *refs):
    corrected, away, kept, parts = refs[chunk_after:]
    step = pl.program_id(0)
    rows = weights.shape[0]
    half = away.shape[0]

    @pl.when(step == 0)
    def _():
        first = core[0] == 0
        top, bottom = warm[:half], warm[half:]
        both = jnp.concatenate([jnp.where(first, bottom, top), jnp.where(first, top, bottom)], axis=0)
        parts[...] = jnp.concatenate(split3(both), axis=0)

    value = weights[...] - copies[0] + error[0]
    here = pl.ds(pl.multiple_of(step * rows, rows), rows)
    corrected[here, :] = value
    left = stacked_product(parts[...], value, ((1,), (1,)))
    away[...] = left[:half]
    kept[...] = left[half:]


def left_call(core, weights, copies, error, warm, after, start, rows, block):
    rank, width = warm.shape
    first = start // block
    row = lambda i: (first + i, 0)
    lead = lambda i: (0, first + i, 0)
    return pl.pallas_call(
        functools.partial(left_kernel, len(after)),
        grid=(rows // block,),
        in_specs=[
            SMEM,
            pl.BlockSpec((block, width), row),
            pl.BlockSpec((1, block, width), lead),
            pl.BlockSpec((1, block, width), lead),
            pl.BlockSpec((rank, width), lambda i: (0, 0)),
        ]
        + [ANY] * len(after),
        out_specs=[
            VMEM,
            pl.BlockSpec((rank // 2, block), lambda i: (0, i)),
            pl.BlockSpec((rank // 2, block), lambda i: (0, i)),
        ],
        out_shape=[
            pltpu.VMEM((rows, width), jnp.float32),
            jax.ShapeDtypeStruct((rank // 2, rows), jnp.float32),
            jax.ShapeDtypeStruct((rank // 2, rows), jnp.float32),
        ],
        scratch_shapes=[pltpu.VMEM((3 * rank, width), jnp.bfloat16)],
        compiler_params=pltpu.CompilerParams(vmem_limit_bytes=26 * MIB),
        name="left",
    )(core, in_hbm(weights), in_hbm(copies), in_hbm(error), in_hbm(warm), *after)


def right_kernel(scale, block, chunk, core, mine, other, corrected, *refs):
    away, kept, left = refs[-3:]
    half, rows = mine.shape
    width = corrected.shape[1]
    first = core[0] == 0
    whole = ordered(first, mine[...] * scale, other[...] * scale)
    left[...] = whole
    parts = jnp.concatenate(split3(whole), axis=0)
    total = None
    for i in range(rows // block):
        cut = slice(i * block, (i + 1) * block)
        here = slice(chunk * rows + i * block, chunk * rows + (i + 1) * block)
        term = stacked_product(parts[:, cut], corrected[here, :], ((1,), (0,)))
        total = term if total is None else total + term
    square = stacked_product(parts, whole, ((1,), (1,)))
    top, bottom = total[:half], total[half:]
    away_value, kept_value = jnp.where(first, bottom, top), jnp.where(first, top, bottom)
    gram = jnp.concatenate([square[:half], square[half:]], axis=1)
    if len(refs) > 3:
        away_before, kept_before = refs[:2]
        away_value = away_value + away_before[:, :width]
        kept_value = kept_value + kept_before[:, :width]
        gram = gram + kept_before[:, width:]
    away[:, :width] = away_value
    away[:, width:] = jnp.zeros_like(gram)
    kept[:, :width] = kept_value
    kept[:, width:] = gram


def right_call(core, mine, other, corrected, before, scale, block, chunk):
    half, rows = mine.shape
    width = corrected.shape[1]
    message = jax.ShapeDtypeStruct((half, width + 4 * half), jnp.float32)
    return pl.pallas_call(
        functools.partial(right_kernel, scale, block, chunk),
        in_specs=[SMEM] + [VMEM] * (3 + len(before)),
        out_specs=[VMEM] * 3,
        out_shape=[message, message, jax.ShapeDtypeStruct((2 * half, rows), jnp.float32)],
        compiler_params=pltpu.CompilerParams(vmem_limit_bytes=12 * MIB),
        name="right",
    )(core, mine, other, in_vmem(corrected), *before)


def factor_kernel(message, *refs):
    chunks = (len(refs) - 1) // 2
    left, inverse, basis = refs[:chunks], refs[chunks], refs[chunks + 1 :]
    half = message.shape[0]
    rank = 2 * half
    pair = message[...]
    gram = jnp.concatenate([pair[:, :rank], pair[:, rank:]], axis=0)
    eye = jnp.where(
        lax.broadcasted_iota(jnp.int32, (rank, rank), 0) == lax.broadcasted_iota(jnp.int32, (rank, rank), 1), 1.0, 0.0
    )
    both = jnp.concatenate([gram, eye], axis=1)
    bands = [both[i : i + 8, :] for i in range(0, rank, 8)]
    group = 4
    for j in range(0, rank, group):
        band, line = divmod(j, 8)
        columns = [
            [jnp.broadcast_to(rest[:, j + k : j + k + 1], rest.shape) for k in range(group)] for rest in bands[band:]
        ]
        rows = [bands[band][line + k : line + k + 1, :] for k in range(group)]
        corner = [[columns[0][m][line + k : line + k + 1, :] for m in range(group)] for k in range(group)]
        roots, factors = [], []
        for k in range(group):
            root = lax.rsqrt(corner[k][k])
            rows[k] = rows[k] * root
            inverse[j + k : j + k + 1, :] = rows[k][:, rank:]
            factor = {m: corner[m][k] * root for m in range(k + 1, group)}
            for m in range(k + 1, group):
                rows[m] = rows[m] - factor[m] * rows[k]
                for n in range(k + 1, m + 1):
                    corner[m][n] = corner[m][n] - factor[m] * factor[n]
            roots.append(root)
            factors.append(factor)
        for k in reversed(range(group)):
            for m in range(k + 1, group):
                rows[k] = rows[k] - factors[k][m] * rows[m]
            rows[k] = rows[k] * roots[k]
        for i in range(band, rank // 8):
            column = columns[i - band]
            bands[i] = bands[i] - (
                (column[0] * rows[0] + column[1] * rows[1]) + (column[2] * rows[2] + column[3] * rows[3])
            )
    for chunk in range(chunks):
        rows = lax.dot_general(
            inverse[...],
            left[chunk][...],
            (((1,), (0,)), ((), ())),
            precision=lax.Precision.HIGHEST,
            preferred_element_type=jnp.float32,
        )
        high, middle, low = split3(rows.T)
        basis[chunk][...] = jnp.concatenate([high, high, middle, high, low, middle], axis=1)


def factor_call(message, left):
    half = message.shape[0]
    rank = 2 * half
    return pl.pallas_call(
        factor_kernel,
        in_specs=[VMEM] * (1 + len(left)),
        out_specs=[VMEM] * (1 + len(left)),
        out_shape=[jax.ShapeDtypeStruct((rank, rank), jnp.float32)]
        + [jax.ShapeDtypeStruct((piece.shape[1], 6 * rank), jnp.bfloat16) for piece in left],
        compiler_params=pltpu.CompilerParams(vmem_limit_bytes=12 * MIB),
        name="factor",
    )(message, *left)


def final_kernel(scale, chunks, core, mine, other, inverse, moment, weights, corrected, *refs):
    basis = refs[:chunks]
    updated, velocity, carried, parts = refs[-4:]
    step = pl.program_id(0)
    rows, width = updated.shape
    here = pl.ds(pl.multiple_of(step * rows, rows), rows)

    @pl.when(step == 0)
    def _():
        whole = ordered(core[0] == 0, mine[:, :width] * scale, other[:, :width] * scale)
        right = lax.dot_general(
            inverse[...], whole, (((1,), (0,)), ((), ())), precision=lax.Precision.HIGHEST, preferred_element_type=jnp.float32
        )
        high, middle, low = split3(right)
        parts[...] = jnp.concatenate([high, middle, high, low, high, middle], axis=0)

    def work(chunk, at):
        there = pl.ds(pl.multiple_of(at, rows), rows)
        change = jnp.dot(basis[chunk][there, :], parts[...], preferred_element_type=jnp.float32)
        carried[0] = corrected[here, :] - change
        new, speed = nesterov(weights[here, :], change, moment[here, :])
        updated[...] = new
        velocity[...] = speed

    first = 0
    for chunk in range(chunks):
        count = basis[chunk].shape[0] // rows
        here_now = jnp.logical_and(step >= first, step < first + count)
        pl.when(here_now)(functools.partial(work, chunk, (step - first) * rows))
        first += count


def final_call(core, mine, other, inverse, moment, weights, corrected, basis, after, scale, block):
    rows, width = moment.shape
    rank = inverse.shape[0]
    chunks = len(basis)
    out = pl.BlockSpec((block, width), lambda i: (i, 0))
    large = [in_vmem(value) for value in (moment, weights, corrected, *basis)]
    return pl.pallas_call(
        functools.partial(final_kernel, scale, chunks),
        grid=(rows // block,),
        in_specs=[SMEM] + [VMEM] * (3 + len(large)) + [ANY] * len(after),
        out_specs=[out, out, pl.BlockSpec((1, block, width), lambda i: (0, i, 0))],
        out_shape=[
            jax.ShapeDtypeStruct((rows, width), jnp.float32),
            jax.ShapeDtypeStruct((rows, width), jnp.float32),
            jax.ShapeDtypeStruct((1, rows, width), jnp.float32),
        ],
        scratch_shapes=[pltpu.VMEM((6 * rank, width), jnp.bfloat16)],
        compiler_params=pltpu.CompilerParams(vmem_limit_bytes=24 * MIB),
        name="final",
    )(core, mine, other, inverse, *large, *after)


def sum_kernel(parts, one, two, *refs):
    width = one.shape[1] // parts
    for i, out in enumerate(refs[len(refs) - parts :]):
        cut = slice(i * width, (i + 1) * width)
        out[...] = one[:, cut] + two[:, cut]


def sum_call(one, two, after, parts=1):
    out = jax.ShapeDtypeStruct((one.shape[0], one.shape[1] // parts), one.dtype)
    return pl.pallas_call(
        functools.partial(sum_kernel, parts),
        in_specs=[VMEM] * 2 + [ANY] * len(after),
        out_specs=VMEM if parts == 1 else [VMEM] * parts,
        out_shape=out if parts == 1 else [out] * parts,
        compiler_params=pltpu.CompilerParams(vmem_limit_bytes=8 * MIB),
        name="sum",
    )(one, two, *after)


def away_kernel(core, weights, copies, *refs):
    refs[-1][...] = weights[0] - copies[0, 0]


def both_kernel(core, weights, copies, received, *refs):
    refs[-1][...] = (weights[0] - copies[0, 0]) + (weights[0] - received[0, 0])


def half_call(kernel, flip, core, weights, copies, after):
    _, rows, width = weights.shape
    block = rows // 2 if rows % 16 == 0 else rows
    pick = (lambda core: 1 - core[0]) if flip else (lambda core: core[0])
    part = pl.BlockSpec((1, block, width), lambda i, core: (pick(core), i, 0))
    whole = pl.BlockSpec((1, 1, block, width), lambda i, core: (0, pick(core), i, 0))
    return pl.pallas_call(
        kernel,
        grid_spec=pltpu.PrefetchScalarGridSpec(
            num_scalar_prefetch=1,
            grid=(rows // block,),
            in_specs=[part] + [whole] * len(copies) + [ANY] * len(after),
            out_specs=pl.BlockSpec((block, width), lambda i, core: (i, 0)),
        ),
        out_shape=jax.ShapeDtypeStruct((rows, width), jnp.float32),
        compiler_params=pltpu.CompilerParams(vmem_limit_bytes=12 * MIB),
        name=kernel.__name__[:-7],
    )(core, in_hbm(weights), in_hbm(copies[0]), *copies[1:], *after)


def term_kernel(core, weights, copies, received, *refs):
    at = core[0]
    refs[-1][...] = (weights[at] - copies[0, at]) + received[...]


def term_call(core, weights, copies, received, after):
    return pl.pallas_call(
        term_kernel,
        in_specs=[SMEM] + [VMEM] * 3 + [ANY] * len(after),
        out_specs=VMEM,
        out_shape=jax.ShapeDtypeStruct(weights.shape[1:], jnp.float32),
        compiler_params=pltpu.CompilerParams(vmem_limit_bytes=12 * MIB),
        name="term",
    )(core, weights, copies, received, *after)


def layer_kernel(scale, core, mine, other, weights, moment, *refs):
    updated, velocity, mark = refs[-3:]
    for value, at in ((mine, core[0]), (other, 1 - core[0])):
        updated[at], velocity[at] = nesterov(weights[at], value[...] * scale, moment[at])
    mark[...] = jnp.zeros_like(mark)


def layer_call(core, mine, other, weights, moment, after, scale):
    return pl.pallas_call(
        functools.partial(layer_kernel, scale),
        in_specs=[SMEM] + [VMEM] * 4 + [ANY] * len(after),
        out_specs=[VMEM] * 3,
        out_shape=[jax.ShapeDtypeStruct(weights.shape, jnp.float32)] * 2 + [jax.ShapeDtypeStruct((8, 128), jnp.float32)],
        compiler_params=pltpu.CompilerParams(vmem_limit_bytes=16 * MIB),
        name="layer",
    )(core, mine, other, weights, moment, *after)


def local(
    square_weights,
    square_copies,
    square_moment,
    broad_weights,
    broad_copies,
    broad_moment,
    embed_weights,
    embed_copies,
    embed_moment,
    embed_error,
    warm_start,
):
    replicas = lax.axis_size("replica")
    scale = 1 / replicas
    rank, width = warm_start.shape
    rows = embed_weights.shape[0]
    core = jnp.reshape(lax.axis_index("replica") & 1, (1,)).astype(jnp.int32)

    square_received = swap(square_copies, "replica", 1)
    broad_away = half_call(away_kernel, True, core, broad_weights, (broad_copies,), ())
    square_half = half_call(both_kernel, False, core, square_weights, (square_copies, square_received), (broad_away,))
    broad_received = swap(broad_away, "replica", 1)
    chunks = 2 if rows % 512 == 0 else 1
    corrected, away, kept = left_call(
        core, embed_weights, embed_copies, embed_error, warm_start, (square_half,), 0, rows, math.gcd(rows, 512)
    )
    square_half = sum_over_chips(square_half, ())
    pair = sum_call(kept, swap(away, "replica", 1), (square_half,), chunks)
    halves, others, ready = [], [], ()
    for piece in pair if chunks > 1 else [pair]:
        halves.append(sum_over_chips(piece, ready))
        others.append(swap(halves[-1], "replica", 1))
        ready = (others[-1],)
    broad_half = term_call(core, broad_weights, broad_copies, broad_received, tuple(halves))
    before, left = [], []
    for chunk, half in enumerate(halves):
        *before, piece = right_call(
            core, half, others[chunk], corrected, before, scale, math.gcd(rows // chunks, 1024), chunk
        )
        left.append(piece)
    away, kept = before

    message = sum_call(kept, swap(away, "replica", 1), ())
    inner = lax.axis_size("inner")
    bit = 1
    while 2 * bit < inner:
        message = sum_call(message, swap(message, "inner", bit), ())
        bit *= 2
    square_other = swap(square_half, "replica", 1)
    received = swap(message, "inner", bit)
    square_updated, square_velocity, mark = layer_call(
        core, square_half, square_other, square_weights, square_moment, (message,), scale
    )
    message, gram = part_call(message, received, (mark,), width)
    inverse, *basis = factor_call(gram, left)
    right_half = sum_over_chips(message, (inverse,))
    broad_half = sum_over_chips(broad_half, (message,))
    broad_other = swap(broad_half, "replica", 1)
    broad_updated, broad_velocity, mark = layer_call(
        core, broad_half, broad_other, broad_weights, broad_moment, (right_half,), scale
    )
    right_other = swap(right_half, "replica", 1)
    embed_updated, embed_velocity, embed_carried = final_call(
        core, right_half, right_other, inverse, embed_moment, embed_weights, corrected, basis, (mark,), scale, math.gcd(rows, 512)
    )
    return (
        square_updated,
        square_velocity,
        broad_updated,
        broad_velocity,
        embed_updated,
        embed_velocity,
        embed_carried,
    )


def solution(mesh):
    in_specs = (
        P(None, "inner", None),
        P("replica", None, "inner", None),
        P(None, "inner", None),
        P(None, "inner", None),
        P("replica", None, "inner", None),
        P(None, "inner", None),
        P("inner", None),
        P("replica", "inner", None),
        P("inner", None),
        P("replica", "inner", None),
        P(),
    )
    out_specs = (
        P(None, "inner", None),
        P(None, "inner", None),
        P(None, "inner", None),
        P(None, "inner", None),
        P("inner", None),
        P("inner", None),
        P("replica", "inner", None),
    )
    return jax.shard_map(local, mesh=mesh, in_specs=in_specs, out_specs=out_specs, check_vma=False)
```

```python
import functools
import math

import jax
import jax.numpy as jnp
from jax import lax
from jax.experimental import pallas as pl
from jax.experimental.pallas import tpu as pltpu
from jax.sharding import PartitionSpec as P

outer_rate = 0.7
momentum_decay = 0.9
MIB = 1 << 20


def nesterov(weights, gradient, moment):
    velocity = momentum_decay * moment + gradient
    return (weights - outer_rate * (gradient + momentum_decay * velocity), velocity)


def split3(value):
    high = value.astype(jnp.bfloat16)
    rest = value - high.astype(jnp.float32)
    middle = rest.astype(jnp.bfloat16)
    low = (rest - middle.astype(jnp.float32)).astype(jnp.bfloat16)
    return high, middle, low


def stacked_product(parts, right, dims):
    rows = parts.shape[0] // 3
    high, middle, low = split3(right)
    dot = functools.partial(lax.dot_general, dimension_numbers=(dims, ((), ())), preferred_element_type=jnp.float32)
    one = dot(parts, high)
    two = dot(parts[: 2 * rows], middle)
    three = dot(parts[:rows], low)
    small = one[2 * rows :] + two[rows:] + three
    return one[:rows] + (one[rows : 2 * rows] + two[:rows] + small)


def swap(value, axis, bit):
    return lax.ppermute(value, axis, [(i, i ^ bit) for i in range(lax.axis_size(axis))])


def doubled(value, axis, first=1):
    bit = first
    while bit < lax.axis_size(axis):
        value = value + swap(value, axis, bit)
        bit *= 2
    return value


def part_kernel(one, two, *refs):
    left, right = refs[-2:]
    width = left.shape[1]
    left[...] = one[:, :width] + two[:, :width]
    right[...] = one[:, width:] + two[:, width:]


def part_call(one, two, after, width):
    rows, total = one.shape
    return pl.pallas_call(
        part_kernel,
        in_specs=[VMEM] * 2 + [ANY] * len(after),
        out_specs=[VMEM] * 2,
        out_shape=[
            jax.ShapeDtypeStruct((rows, width), jnp.float32),
            jax.ShapeDtypeStruct((rows, total - width), jnp.float32),
        ],
        compiler_params=pltpu.CompilerParams(vmem_limit_bytes=8 * MIB),
        name="part",
    )(one, two, *after)


def sum_over_chips(value, after):
    bit = 2
    while bit < lax.axis_size("replica"):
        value = sum_call(value, swap(value, "replica", bit), after)
        bit *= 2
    return value


def in_hbm(value):
    return pltpu.with_memory_space_constraint(value, pltpu.HBM)


def in_vmem(value):
    return pltpu.with_memory_space_constraint(value, pltpu.VMEM)


VMEM = pl.BlockSpec(memory_space=pltpu.VMEM)
SMEM = pl.BlockSpec(memory_space=pltpu.SMEM)
ANY = pl.BlockSpec(memory_space=pl.ANY)


def ordered(first, mine, other):
    return jnp.concatenate([jnp.where(first, mine, other), jnp.where(first, other, mine)], axis=0)


def left_kernel(chunk_after, core, weights, copies, error, warm, *refs):
    corrected, away, kept, parts = refs[chunk_after:]
    step = pl.program_id(0)
    rows = weights.shape[0]
    half = away.shape[0]

    @pl.when(step == 0)
    def _():
        first = core[0] == 0
        top, bottom = warm[:half], warm[half:]
        both = jnp.concatenate([jnp.where(first, bottom, top), jnp.where(first, top, bottom)], axis=0)
        parts[...] = jnp.concatenate(split3(both), axis=0)

    value = weights[...] - copies[0] + error[0]
    here = pl.ds(pl.multiple_of(step * rows, rows), rows)
    corrected[here, :] = value
    left = stacked_product(parts[...], value, ((1,), (1,)))
    away[...] = left[:half]
    kept[...] = left[half:]


def left_call(core, weights, copies, error, warm, after, start, rows, block):
    rank, width = warm.shape
    first = start // block
    row = lambda i: (first + i, 0)
    lead = lambda i: (0, first + i, 0)
    return pl.pallas_call(
        functools.partial(left_kernel, len(after)),
        grid=(rows // block,),
        in_specs=[
            SMEM,
            pl.BlockSpec((block, width), row),
            pl.BlockSpec((1, block, width), lead),
            pl.BlockSpec((1, block, width), lead),
            pl.BlockSpec((rank, width), lambda i: (0, 0)),
        ]
        + [ANY] * len(after),
        out_specs=[
            VMEM,
            pl.BlockSpec((rank // 2, block), lambda i: (0, i)),
            pl.BlockSpec((rank // 2, block), lambda i: (0, i)),
        ],
        out_shape=[
            pltpu.VMEM((rows, width), jnp.float32),
            jax.ShapeDtypeStruct((rank // 2, rows), jnp.float32),
            jax.ShapeDtypeStruct((rank // 2, rows), jnp.float32),
        ],
        scratch_shapes=[pltpu.VMEM((3 * rank, width), jnp.bfloat16)],
        compiler_params=pltpu.CompilerParams(vmem_limit_bytes=26 * MIB),
        name="left",
    )(core, in_hbm(weights), in_hbm(copies), in_hbm(error), in_hbm(warm), *after)


def right_kernel(scale, block, chunk, core, mine, other, corrected, *refs):
    away, kept, left = refs[-3:]
    half, rows = mine.shape
    width = corrected.shape[1]
    first = core[0] == 0
    whole = ordered(first, mine[...] * scale, other[...] * scale)
    left[...] = whole
    parts = jnp.concatenate(split3(whole), axis=0)
    total = None
    for i in range(rows // block):
        cut = slice(i * block, (i + 1) * block)
        here = slice(chunk * rows + i * block, chunk * rows + (i + 1) * block)
        term = stacked_product(parts[:, cut], corrected[here, :], ((1,), (0,)))
        total = term if total is None else total + term
    square = stacked_product(parts, whole, ((1,), (1,)))
    top, bottom = total[:half], total[half:]
    away_value, kept_value = jnp.where(first, bottom, top), jnp.where(first, top, bottom)
    gram = jnp.concatenate([square[:half], square[half:]], axis=1)
    if len(refs) > 3:
        away_before, kept_before = refs[:2]
        away_value = away_value + away_before[:, :width]
        kept_value = kept_value + kept_before[:, :width]
        gram = gram + kept_before[:, width:]
    away[:, :width] = away_value
    away[:, width:] = jnp.zeros_like(gram)
    kept[:, :width] = kept_value
    kept[:, width:] = gram


def right_call(core, mine, other, corrected, before, scale, block, chunk):
    half, rows = mine.shape
    width = corrected.shape[1]
    message = jax.ShapeDtypeStruct((half, width + 4 * half), jnp.float32)
    return pl.pallas_call(
        functools.partial(right_kernel, scale, block, chunk),
        in_specs=[SMEM] + [VMEM] * (3 + len(before)),
        out_specs=[VMEM] * 3,
        out_shape=[message, message, jax.ShapeDtypeStruct((2 * half, rows), jnp.float32)],
        compiler_params=pltpu.CompilerParams(vmem_limit_bytes=12 * MIB),
        name="right",
    )(core, mine, other, in_vmem(corrected), *before)


def factor_kernel(message, *refs):
    chunks = (len(refs) - 1) // 2
    left, inverse, basis = refs[:chunks], refs[chunks], refs[chunks + 1 :]
    half = message.shape[0]
    rank = 2 * half
    pair = message[...]
    gram = jnp.concatenate([pair[:, :rank], pair[:, rank:]], axis=0)
    eye = jnp.where(
        lax.broadcasted_iota(jnp.int32, (rank, rank), 0) == lax.broadcasted_iota(jnp.int32, (rank, rank), 1), 1.0, 0.0
    )
    both = jnp.concatenate([gram, eye], axis=1)
    bands = [both[i : i + 8, :] for i in range(0, rank, 8)]
    group = 4
    for j in range(0, rank, group):
        band, line = divmod(j, 8)
        columns = [
            [jnp.broadcast_to(rest[:, j + k : j + k + 1], rest.shape) for k in range(group)] for rest in bands[band:]
        ]
        rows = [bands[band][line + k : line + k + 1, :] for k in range(group)]
        corner = [[columns[0][m][line + k : line + k + 1, :] for m in range(group)] for k in range(group)]
        roots, factors = [], []
        for k in range(group):
            root = lax.rsqrt(corner[k][k])
            rows[k] = rows[k] * root
            inverse[j + k : j + k + 1, :] = rows[k][:, rank:]
            factor = {m: corner[m][k] * root for m in range(k + 1, group)}
            for m in range(k + 1, group):
                rows[m] = rows[m] - factor[m] * rows[k]
                for n in range(k + 1, m + 1):
                    corner[m][n] = corner[m][n] - factor[m] * factor[n]
            roots.append(root)
            factors.append(factor)
        for k in reversed(range(group)):
            for m in range(k + 1, group):
                rows[k] = rows[k] - factors[k][m] * rows[m]
            rows[k] = rows[k] * roots[k]
        for i in range(band, rank // 8):
            column = columns[i - band]
            bands[i] = bands[i] - (
                (column[0] * rows[0] + column[1] * rows[1]) + (column[2] * rows[2] + column[3] * rows[3])
            )
    for chunk in range(chunks):
        rows = lax.dot_general(
            inverse[...],
            left[chunk][...],
            (((1,), (0,)), ((), ())),
            precision=lax.Precision.HIGHEST,
            preferred_element_type=jnp.float32,
        )
        high, middle, low = split3(rows.T)
        basis[chunk][...] = jnp.concatenate([high, high, middle, high, low, middle], axis=1)


def factor_call(message, left):
    half = message.shape[0]
    rank = 2 * half
    return pl.pallas_call(
        factor_kernel,
        in_specs=[VMEM] * (1 + len(left)),
        out_specs=[VMEM] * (1 + len(left)),
        out_shape=[jax.ShapeDtypeStruct((rank, rank), jnp.float32)]
        + [jax.ShapeDtypeStruct((piece.shape[1], 6 * rank), jnp.bfloat16) for piece in left],
        compiler_params=pltpu.CompilerParams(vmem_limit_bytes=12 * MIB),
        name="factor",
    )(message, *left)


def final_kernel(scale, chunks, core, mine, other, inverse, moment, weights, corrected, *refs):
    basis = refs[:chunks]
    updated, velocity, carried, parts = refs[-4:]
    step = pl.program_id(0)
    rows, width = updated.shape
    here = pl.ds(pl.multiple_of(step * rows, rows), rows)

    @pl.when(step == 0)
    def _():
        whole = ordered(core[0] == 0, mine[:, :width] * scale, other[:, :width] * scale)
        right = lax.dot_general(
            inverse[...], whole, (((1,), (0,)), ((), ())), precision=lax.Precision.HIGHEST, preferred_element_type=jnp.float32
        )
        high, middle, low = split3(right)
        parts[...] = jnp.concatenate([high, middle, high, low, high, middle], axis=0)

    def work(chunk, at):
        there = pl.ds(pl.multiple_of(at, rows), rows)
        change = jnp.dot(basis[chunk][there, :], parts[...], preferred_element_type=jnp.float32)
        carried[0] = corrected[here, :] - change
        new, speed = nesterov(weights[here, :], change, moment[here, :])
        updated[...] = new
        velocity[...] = speed

    first = 0
    for chunk in range(chunks):
        count = basis[chunk].shape[0] // rows
        here_now = jnp.logical_and(step >= first, step < first + count)
        pl.when(here_now)(functools.partial(work, chunk, (step - first) * rows))
        first += count


def final_call(core, mine, other, inverse, moment, weights, corrected, basis, after, scale, block):
    rows, width = moment.shape
    rank = inverse.shape[0]
    chunks = len(basis)
    out = pl.BlockSpec((block, width), lambda i: (i, 0))
    large = [in_vmem(value) for value in (moment, weights, corrected, *basis)]
    return pl.pallas_call(
        functools.partial(final_kernel, scale, chunks),
        grid=(rows // block,),
        in_specs=[SMEM] + [VMEM] * (3 + len(large)) + [ANY] * len(after),
        out_specs=[out, out, pl.BlockSpec((1, block, width), lambda i: (0, i, 0))],
        out_shape=[
            jax.ShapeDtypeStruct((rows, width), jnp.float32),
            jax.ShapeDtypeStruct((rows, width), jnp.float32),
            jax.ShapeDtypeStruct((1, rows, width), jnp.float32),
        ],
        scratch_shapes=[pltpu.VMEM((6 * rank, width), jnp.bfloat16)],
        compiler_params=pltpu.CompilerParams(vmem_limit_bytes=24 * MIB),
        name="final",
    )(core, mine, other, inverse, *large, *after)


def sum_kernel(parts, one, two, *refs):
    width = one.shape[1] // parts
    for i, out in enumerate(refs[len(refs) - parts :]):
        cut = slice(i * width, (i + 1) * width)
        out[...] = one[:, cut] + two[:, cut]


def sum_call(one, two, after, parts=1):
    out = jax.ShapeDtypeStruct((one.shape[0], one.shape[1] // parts), one.dtype)
    return pl.pallas_call(
        functools.partial(sum_kernel, parts),
        in_specs=[VMEM] * 2 + [ANY] * len(after),
        out_specs=VMEM if parts == 1 else [VMEM] * parts,
        out_shape=out if parts == 1 else [out] * parts,
        compiler_params=pltpu.CompilerParams(vmem_limit_bytes=8 * MIB),
        name="sum",
    )(one, two, *after)


def split_kernel(core, weights, copies, away, kept):
    at = core[0]
    away[...] = weights[1 - at] - copies[0, 1 - at]
    kept[...] = weights[at] - copies[0, at]


def split_call(core, weights, copies):
    _, rows, width = weights.shape
    block = rows // 4 if rows % 32 == 0 else rows
    out = pl.BlockSpec((block, width), lambda i: (i, 0))
    return pl.pallas_call(
        split_kernel,
        grid=(rows // block,),
        in_specs=[
            SMEM,
            pl.BlockSpec((2, block, width), lambda i: (0, i, 0)),
            pl.BlockSpec((1, 2, block, width), lambda i: (0, 0, i, 0)),
        ],
        out_specs=[out, out],
        out_shape=[jax.ShapeDtypeStruct((rows, width), jnp.float32)] * 2,
        compiler_params=pltpu.CompilerParams(vmem_limit_bytes=12 * MIB),
        name="split",
    )(core, in_hbm(weights), in_hbm(copies))


def both_kernel(core, weights, copies, received, *refs):
    refs[-1][...] = (weights[0] - copies[0, 0]) + (weights[0] - received[0, 0])


def half_call(kernel, flip, core, weights, copies, after):
    _, rows, width = weights.shape
    block = rows // 2 if rows % 16 == 0 else rows
    pick = (lambda core: 1 - core[0]) if flip else (lambda core: core[0])
    part = pl.BlockSpec((1, block, width), lambda i, core: (pick(core), i, 0))
    whole = pl.BlockSpec((1, 1, block, width), lambda i, core: (0, pick(core), i, 0))
    return pl.pallas_call(
        kernel,
        grid_spec=pltpu.PrefetchScalarGridSpec(
            num_scalar_prefetch=1,
            grid=(rows // block,),
            in_specs=[part] + [whole] * len(copies) + [ANY] * len(after),
            out_specs=pl.BlockSpec((block, width), lambda i, core: (i, 0)),
        ),
        out_shape=jax.ShapeDtypeStruct((rows, width), jnp.float32),
        compiler_params=pltpu.CompilerParams(vmem_limit_bytes=12 * MIB),
        name=kernel.__name__[:-7],
    )(core, in_hbm(weights), in_hbm(copies[0]), *copies[1:], *after)


def layer_kernel(scale, core, mine, other, weights, moment, *refs):
    updated, velocity, mark = refs[-3:]
    for value, at in ((mine, core[0]), (other, 1 - core[0])):
        updated[at], velocity[at] = nesterov(weights[at], value[...] * scale, moment[at])
    mark[...] = jnp.zeros_like(mark)


def layer_call(core, mine, other, weights, moment, after, scale):
    return pl.pallas_call(
        functools.partial(layer_kernel, scale),
        in_specs=[SMEM] + [VMEM] * 4 + [ANY] * len(after),
        out_specs=[VMEM] * 3,
        out_shape=[jax.ShapeDtypeStruct(weights.shape, jnp.float32)] * 2 + [jax.ShapeDtypeStruct((8, 128), jnp.float32)],
        compiler_params=pltpu.CompilerParams(vmem_limit_bytes=16 * MIB),
        name="layer",
    )(core, mine, other, weights, moment, *after)


def local(
    square_weights,
    square_copies,
    square_moment,
    broad_weights,
    broad_copies,
    broad_moment,
    embed_weights,
    embed_copies,
    embed_moment,
    embed_error,
    warm_start,
):
    replicas = lax.axis_size("replica")
    scale = 1 / replicas
    rank, width = warm_start.shape
    rows = embed_weights.shape[0]
    core = jnp.reshape(lax.axis_index("replica") & 1, (1,)).astype(jnp.int32)

    square_received = swap(square_copies, "replica", 1)
    broad_away, broad_kept = split_call(core, broad_weights, broad_copies)
    square_half = half_call(both_kernel, False, core, square_weights, (square_copies, square_received), (broad_away,))
    broad_received = swap(broad_away, "replica", 1)
    chunks = 2 if rows % 512 == 0 else 1
    corrected, away, kept = left_call(
        core, embed_weights, embed_copies, embed_error, warm_start, (square_half,), 0, rows, math.gcd(rows, 512)
    )
    square_half = sum_over_chips(square_half, ())
    pair = sum_call(kept, swap(away, "replica", 1), (square_half,), chunks)
    halves, others, ready = [], [], ()
    for piece in pair if chunks > 1 else [pair]:
        halves.append(sum_over_chips(piece, ready))
        others.append(swap(halves[-1], "replica", 1))
        ready = (others[-1],)
    broad_half = sum_call(broad_kept, broad_received, tuple(halves))
    before, left = [], []
    for chunk, half in enumerate(halves):
        *before, piece = right_call(
            core, half, others[chunk], corrected, before, scale, math.gcd(rows // chunks, 256), chunk
        )
        left.append(piece)
    away, kept = before

    message = sum_call(kept, swap(away, "replica", 1), ())
    inner = lax.axis_size("inner")
    bit = 1
    while 2 * bit < inner:
        message = sum_call(message, swap(message, "inner", bit), ())
        bit *= 2
    square_other = swap(square_half, "replica", 1)
    received = swap(message, "inner", bit)
    square_updated, square_velocity, mark = layer_call(
        core, square_half, square_other, square_weights, square_moment, (message,), scale
    )
    message, gram = part_call(message, received, (mark,), width)
    inverse, *basis = factor_call(gram, left)
    right_half = sum_over_chips(message, (inverse,))
    broad_half = sum_over_chips(broad_half, (message,))
    broad_other = swap(broad_half, "replica", 1)
    broad_updated, broad_velocity, mark = layer_call(
        core, broad_half, broad_other, broad_weights, broad_moment, (right_half,), scale
    )
    right_other = swap(right_half, "replica", 1)
    embed_updated, embed_velocity, embed_carried = final_call(
        core, right_half, right_other, inverse, embed_moment, embed_weights, corrected, basis, (mark,), scale, math.gcd(rows, 512)
    )
    return (
        square_updated,
        square_velocity,
        broad_updated,
        broad_velocity,
        embed_updated,
        embed_velocity,
        embed_carried,
    )


def solution(mesh):
    in_specs = (
        P(None, "inner", None),
        P("replica", None, "inner", None),
        P(None, "inner", None),
        P(None, "inner", None),
        P("replica", None, "inner", None),
        P(None, "inner", None),
        P("inner", None),
        P("replica", "inner", None),
        P("inner", None),
        P("replica", "inner", None),
        P(),
    )
    out_specs = (
        P(None, "inner", None),
        P(None, "inner", None),
        P(None, "inner", None),
        P(None, "inner", None),
        P("inner", None),
        P("inner", None),
        P("replica", "inner", None),
    )
    return jax.shard_map(local, mesh=mesh, in_specs=in_specs, out_specs=out_specs, check_vma=False)
```
